256 devices in a mesh: pb: 16 (over y, z_hi), ka: 16 (over z_lo, x, core).
Axes of the slice: x: 4, y: 4, z: 8 (z_hi: 4, z_lo: 2; z = z_hi * 2 + z_lo), core: 2. Of those that a mesh axis runs over, the one named last changes fastest.
Arguments:
- queries: bfloat16 [16384, 1024], P(('pb', 'ka')), may hold values from -6 to 6
- key_vecs: bfloat16 [16384, 128], P(('pb', 'ka')), may hold values from -6 to 6
- value_vecs: bfloat16 [16384, 128], P(('pb', 'ka')), may hold values from -6 to 6
- outputs: bfloat16 [16384, 1024], P(('pb', 'ka')), may hold values from -6 to 6
- out_grad: bfloat16 [16384, 1024], P(('pb', 'ka')), may hold values from -6 to 6
- positions: int32 [16384], replicated, may hold values from 0 to 16383, as said below
Outputs:
- query_grad: bfloat16 [16384, 1024], P(('pb', 'ka'))
- key_grad: bfloat16 [16384, 128], P(('pb', 'ka'))
- value_grad: bfloat16 [16384, 128], P(('pb', 'ka'))
The draws below stay inside these ranges and needn't reach their ends.
Inputs may be any that keep to these rules, and one draw needn't show every extreme that they name: Each aligned run of 128 rows holds 128 consecutive positions in increasing order, and the runs together hold every position of the trace once.
All inputs are finite; a program needn't handle non-finite values.
Results may differ from the reference program's by a relative error of at most 0.0051.
Values may be sent and summed in bfloat16 or wider, within the bound.
A program may use at most 64 MiB of HBM per device.

```python
import jax
import jax.numpy as jnp
from jax import lax

HEADS = 8
HD = 128
BLOCK = 128
SEQ = 16384


def draw_queries(key, part):
    key = jax.random.fold_in(key, 11)
    base = jax.random.truncated_normal(key, -6.0, 6.0, (SEQ, HEADS * HD), jnp.float32)
    return base.astype(jnp.bfloat16)


def draw_key_vecs(key, part):
    key = jax.random.fold_in(key, 12)
    base = jax.random.truncated_normal(key, -6.0, 6.0, (SEQ, HD), jnp.float32)
    return base.astype(jnp.bfloat16)


def draw_positions(key, part):
    key = jax.random.fold_in(key, 13)
    order = jax.random.permutation(key, SEQ // BLOCK).astype(jnp.int32)
    within = jnp.arange(BLOCK, dtype=jnp.int32)
    return (order[:, None] * BLOCK + within[None, :]).reshape(SEQ).astype(jnp.int32)


def levels(rng, shape, split, low, top_value):
    loudness = 1.0
    for axis_at, parts in split:
        heights = jax.random.uniform(jax.random.fold_in(jax.random.fold_in(rng, 6), axis_at), (parts,), jnp.float32, low / len(split), top_value / len(split))
        loudness = loudness * jnp.repeat(jnp.exp(heights), shape[axis_at] // parts).reshape((-1,) + (1,) * (len(shape) - 1 - axis_at))
    return loudness


def scatter_about(own_key, dims, deviation, most, split=(), held_as=jnp.bfloat16):
    level = levels(own_key, dims, split, -0.22, 0.18) if split else 1.0
    array = jax.random.normal(own_key, dims, jnp.float32) * deviation * level
    return jnp.minimum(jnp.maximum(array, -most), most).astype(held_as)


def setup_inputs(seed: int = 0) -> dict:
    splits = jax.random.split(jax.random.key(seed), 7)
    return {
        "queries": draw_queries(jax.random.fold_in(splits[6], 71), 0),
        "key_vecs": draw_key_vecs(jax.random.fold_in(splits[6], 71), 0),
        "value_vecs": scatter_about(splits[2], (SEQ, HD), 1.0, 6.0, ((0, 256),)),
        "outputs": scatter_about(splits[3], (SEQ, HEADS * HD), 1.0, 6.0, ((0, 256),)),
        "out_grad": scatter_about(splits[4], (SEQ, HEADS * HD), 1.0, 6.0, ((0, 256),)),
        "positions": draw_positions(jax.random.fold_in(splits[6], 71), 0),
    }


NEG_BIG = -1e30


def reference(queries, key_vecs, value_vecs, outputs, out_grad, positions):
    f32 = jnp.float32
    scaling = HD ** -0.5
    width = min(512, SEQ)
    count = SEQ // width
    query_blocks = queries.reshape(count, width, HEADS, HD)
    output_blocks = outputs.reshape(count, width, HEADS, HD)
    grad_blocks = out_grad.reshape(count, width, HEADS, HD)
    pos_blocks = positions.reshape(count, width)
    key_f = key_vecs.astype(f32)
    value_f = value_vecs.astype(f32)

    def step(carry, block):
        key_acc, value_acc = carry
        query_b, output_b, grad_b, pos_b = block
        query_f = query_b.astype(f32)
        grad_f = grad_b.astype(f32)
        output_f = output_b.astype(f32)
        raw = jnp.einsum("ahd,bd->hab", query_f, key_f) * scaling
        visible = positions[None, None, :] <= pos_b[None, :, None]
        masked = jnp.where(visible, raw, NEG_BIG)
        row_max = jnp.max(masked, axis=2)
        row_sum = jnp.sum(jnp.where(visible, jnp.exp(masked - row_max[:, :, None]), 0.0), axis=2)
        log_norm = row_max + jnp.log(row_sum)
        probs = jnp.where(visible, jnp.exp(masked - log_norm[:, :, None]), 0.0)
        probs_half = lax.optimization_barrier(probs.astype(jnp.bfloat16)).astype(f32)
        delta = jnp.einsum("ahd,ahd->ha", output_f, grad_f)
        dprob = jnp.einsum("ahd,bd->hab", grad_f, value_f)
        dscore = lax.optimization_barrier((probs * (dprob - delta[:, :, None])).astype(jnp.bfloat16)).astype(f32)
        query_part = jnp.einsum("hab,bd->ahd", dscore, key_f) * scaling
        query_part = query_part.astype(jnp.bfloat16).reshape(width, HEADS * HD)
        key_acc = key_acc + jnp.einsum("hab,ahd->bd", dscore, query_f)
        value_acc = value_acc + jnp.einsum("hab,ahd->bd", probs_half, grad_f)
        return (key_acc, value_acc), query_part

    start = (jnp.zeros((SEQ, HD), f32), jnp.zeros((SEQ, HD), f32))
    (key_acc, value_acc), query_parts = lax.scan(step, start, (query_blocks, output_blocks, grad_blocks, pos_blocks))
    query_grad = query_parts.reshape(SEQ, HEADS * HD)
    return (query_grad, (key_acc * scaling).astype(jnp.bfloat16), value_acc.astype(jnp.bfloat16))
```

```python
import math

import jax
import jax.numpy as jnp
from jax import lax
from jax.experimental import pallas as pl
from jax.experimental.pallas import tpu as pltpu
from jax.sharding import PartitionSpec as P

HEADS = 8
HD = 128
NX, NY, NZ, NC = 4, 4, 8, 2
ROWS = 64
WIDE = HEADS * ROWS
COLS = NX * WIDE
TILE = NC * NY * ROWS
HALF = NY * ROWS

HIDDEN = -1e30
FLOOR = -1e20
SCALE = HD ** -0.5
LOG2E = math.log2(math.e)

f32 = jnp.float32
bf16 = jnp.bfloat16
MESH = pl.DeviceIdType.MESH


def dot(left, right, cl, cr):
    return lax.dot_general(
        left, right, (((cl,), (cr,)), ((), ())), preferred_element_type=f32
    )


def where_is(x, y, z, c):
    return {"pb": y * 4 + z // 2, "ka": (z % 2) * 8 + x * 2 + c}


def shard_of(x, y, z, c):
    return (y * 4 + z // 2) * 16 + (z % 2) * 8 + x * 2 + c


def offset_of(j):
    return ((j + 1) // 2) * (2 * (j % 2) - 1)


def kernel(
    starts, q_in, k_in, v_in, o_in, d_in,
    dq_out, dk_out, dv_out,
    q_all, d_all, delta, lse_own, lse_got, lse,
    k_all, v_all, k_pos, q_pos,
    s_even, s_odd, top, total,
    dq_acc, dq_send, dq_got, stage,
    own, core_send, core_got, y_send, y_got, z_send, z_got,
    qs, qr, ds, dr, es, er, ls, lr, gs, gr,
    kzs, kzr, kys, kyr, kcs, kcr,
    vzs, vzr, vys, vyr, vcs, vcr,
    pcs, pcr, pys, pyr, pzs, pzr,
):
    pb, ka = lax.axis_index("pb"), lax.axis_index("ka")
    y = pb // 4
    z = (pb % 4) * 2 + ka // 8
    x = (ka // 2) % 4
    c = ka % 2

    def send(src, dst, ssem, rsem, to):
        return pltpu.make_async_remote_copy(
            src_ref=src, dst_ref=dst, send_sem=ssem, recv_sem=rsem,
            device_id=to, device_id_type=MESH,
        )

    core_peer = where_is(x, y, z, 1 - c)

    def x_peer(e):
        return where_is((x + e) % NX, y, z, c)

    def y_peer(e):
        return where_is(x, (y + e) % NY, z, c)

    def z_peer(e):
        return where_is(x, y, (z + e) % NZ, c)

    barrier = pltpu.get_barrier_semaphore()
    peers = [core_peer]
    peers += [x_peer(e) for e in range(1, NX)]
    peers += [y_peer(e) for e in range(1, NY)]
    peers += [z_peer(e) for e in range(1, NZ)]
    for peer in peers:
        pl.semaphore_signal(barrier, inc=1, device_id=peer, device_id_type=MESH)

    q = q_in[...]
    d = d_in[...]
    for h in range(HEADS):
        rows = pl.ds(h * ROWS, ROWS)
        q_all[x, rows, :] = q[:, h * HD:(h + 1) * HD]
        d_all[x, rows, :] = d[:, h * HD:(h + 1) * HD]
    k_all[z, c, y] = k_in[...]
    v_all[z, c, y] = v_in[...]

    pl.semaphore_wait(barrier, len(peers))

    def q_copy(e):
        return send(q_all.at[x], q_all.at[x], qs.at[e - 1], qr.at[e - 1], x_peer(e))

    def d_copy(e):
        return send(d_all.at[x], d_all.at[x], ds.at[e - 1], dr.at[e - 1], x_peer(e))

    def e_copy(e):
        return send(delta.at[x], delta.at[x], es.at[e - 1], er.at[e - 1], x_peer(e))

    def l_copy(e):
        return send(lse_own, lse_got.at[e - 1], ls.at[e - 1], lr.at[e - 1], x_peer(e))

    def g_copy(e):
        return send(dq_send.at[e - 1], dq_got.at[e - 1], gs.at[e - 1], gr.at[e - 1], x_peer(e))

    def kz_copy(e):
        own_k = k_all.at[z, c, y]
        return send(own_k, own_k, kzs.at[e - 1], kzr.at[e - 1], z_peer(e))

    def vz_copy(e):
        own_v = v_all.at[z, c, y]
        return send(own_v, own_v, vzs.at[e - 1], vzr.at[e - 1], z_peer(e))

    def ky_copy(j, e):
        part = k_all.at[(z + offset_of(j) + NZ) % NZ, c, y]
        return send(part, part, kys.at[j, e - 1], kyr.at[j, e - 1], y_peer(e))

    def vy_copy(j, e):
        part = v_all.at[(z + offset_of(j) + NZ) % NZ, c, y]
        return send(part, part, vys.at[j, e - 1], vyr.at[j, e - 1], y_peer(e))

    def kc_copy(j):
        part = k_all.at[(z + offset_of(j) + NZ) % NZ, c]
        return send(part, part, kcs.at[j], kcr.at[j], core_peer)

    def vc_copy(j):
        part = v_all.at[(z + offset_of(j) + NZ) % NZ, c]
        return send(part, part, vcs.at[j], vcr.at[j], core_peer)

    for e in range(1, NX):
        q_copy(e).start()
    for e in (1, 7, 2, 6, 3, 5, 4):
        kz_copy(e).start()
    for e in range(1, NY):
        ky_copy(0, e).start()
    for e in (1, 7, 2, 6, 3, 5, 4):
        vz_copy(e).start()
    for e in range(1, NY):
        vy_copy(0, e).start()

    o = o_in[...].astype(f32) * d.astype(f32)
    prod = jnp.concatenate([o[:, h * HD:(h + 1) * HD] for h in range(HEADS)], axis=0)
    high = prod.astype(bf16)
    low = (prod - high.astype(f32)).astype(bf16)
    ones = jnp.ones((8, HD), bf16)
    delta[x] = dot(ones, high, 1, 1) + dot(ones, low, 1, 1)

    row = lax.broadcasted_iota(jnp.int32, (ROWS, HD), 0)
    lane = lax.broadcasted_iota(jnp.int32, (8, WIDE), 1) % ROWS

    def place_keys(n, _):
        j, cc, yy = n // (NC * NY), (n // NY) % NC, n % NY
        zz = (z + offset_of(j) + NZ) % NZ
        at = pl.ds(pl.multiple_of(n * ROWS, ROWS), ROWS)
        k_pos[at, :] = row + starts[shard_of(x, yy, zz, cc)]
        return 0

    lax.fori_loop(0, NZ * NC * NY, place_keys, 0)
    for xx in range(NX):
        q_pos[:, xx * WIDE:(xx + 1) * WIDE] = lane + starts[shard_of(xx, y, z, c)]

    top[...] = jnp.full_like(top, FLOOR)
    total[...] = jnp.zeros_like(total)
    dq_acc[...] = jnp.zeros_like(dq_acc)

    def forward_keys(j, _):
        arrived = (NZ - offset_of(j)) % NZ
        kz_copy(arrived).wait_recv()
        for e in range(1, NY):
            ky_copy(j, e).start()
        return 0

    lax.fori_loop(1, NZ, forward_keys, 0)

    def share_keys(j):
        for e in range(1, NY):
            ky_copy(j, e).wait_recv()
        kc_copy(j).start()

    share_keys(0)
    for e in range(1, NX):
        q_copy(e).wait_recv()
    for e in range(1, NX):
        d_copy(e).start()
        e_copy(e).start()

    def arrive(j):
        @pl.when(j < NZ - 1)
        def _():
            share_keys(j + 1)
            vz_copy((NZ - offset_of(j + 1)) % NZ).wait_recv()
            for e in range(1, NY):
                vy_copy(j + 1, e).start()

        kc_copy(j).wait_recv()

    def scores(j, store, t):
        zz = (z + offset_of(j) + NZ) % NZ
        keys = k_all[zz].reshape(TILE, HD)
        queries = q_all[...].reshape(COLS, HD)
        raw = dot(keys, queries, 1, 1) * (SCALE * LOG2E)
        at = pl.ds(pl.multiple_of(j * TILE, TILE), TILE)
        spot = jnp.concatenate([k_pos[at, :]] * (COLS // HD), axis=1)
        raw = jnp.where(spot <= q_pos[0:1, :], raw, HIDDEN)
        store[t] = raw
        return jnp.max(raw.reshape(TILE // 8, 8, COLS), axis=0)

    def sums(store, t, high):
        part = store[t].reshape(TILE // 8, 8, COLS)
        return jnp.sum(jnp.exp2(part - high[None]), axis=0)

    arrive(0)
    top[...] = jnp.maximum(top[...], scores(0, s_even, 0))

    def pair(t, _):
        high = top[...]
        arrive(2 * t + 1)
        seen = scores(2 * t + 1, s_odd, t)
        run = total[...] + sums(s_even, t, high)
        new = jnp.maximum(high, seen)
        total[...] = run * jnp.exp2(high - new)
        top[...] = new

        @pl.when(t < NZ // 2 - 1)
        def _():
            high = top[...]
            arrive(2 * t + 2)
            seen = scores(2 * t + 2, s_even, t + 1)
            run = total[...] + sums(s_odd, t, high)
            new = jnp.maximum(high, seen)
            total[...] = run * jnp.exp2(high - new)
            top[...] = new

        return 0

    lax.fori_loop(0, NZ // 2, pair, 0)
    high = top[...]
    run = total[...] + sums(s_odd, NZ // 2 - 1, high)
    peak = jnp.max(high, axis=0, keepdims=True)
    mass = jnp.sum(run * jnp.exp2(high - peak), axis=0, keepdims=True)
    mine = jnp.where(mass > 0.0, peak + jnp.log2(mass), FLOOR)
    for n in range(8):
        lse_own[n:n + 1, :] = mine[:, n * 256:(n + 1) * 256]
    for e in range(1, NX):
        l_copy(e).start()

    def share_values(j, _):
        for e in range(1, NY):
            vy_copy(j, e).wait_recv()
        vc_copy(j).start()
        return 0

    lax.fori_loop(0, NZ, share_values, 0)

    for e in range(1, NX):
        l_copy(e).wait_recv()
    parts = [lse_own[...]] + [lse_got[e] for e in range(NX - 1)]
    peak = jnp.maximum(jnp.maximum(parts[0], parts[1]), jnp.maximum(parts[2], parts[3]))
    mass = sum(jnp.exp2(part - peak) for part in parts)
    joint = peak + jnp.log2(mass)
    for n in range(8):
        lse[:, n * 256:(n + 1) * 256] = joint[n:n + 1, :]
    for e in range(1, NX):
        d_copy(e).wait_recv()
        e_copy(e).wait_recv()

    def pc_copy(i):
        return send(core_send.at[i], core_got.at[i], pcs.at[i], pcr.at[i], core_peer)

    def py_copy(i, e):
        return send(
            y_send.at[i, (y + e) % NY], y_got.at[i, e - 1],
            pys.at[i, e - 1], pyr.at[i, e - 1], y_peer(e),
        )

    def pz_copy(i, e):
        return send(z_send.at[i], z_got.at[e - 1], pzs.at[e - 1], pzr.at[e - 1], z_peer(e))

    def fold_core(i):
        pc_copy(i).wait_recv()
        both = own[i] + core_got[i].astype(f32)
        y_send[i] = both.astype(bf16).reshape(NY, ROWS, 2 * HD)
        for e in range(1, NY):
            py_copy(i, e).start()

    def fold_y(i):
        for e in range(1, NY):
            py_copy(i, e).wait_recv()
        part = y_send[i, y].astype(f32)
        for e in range(NY - 1):
            part = part + y_got[i, e].astype(f32)
        return part

    def send_z(i):
        z_send[i] = fold_y(i).astype(bf16)
        pz_copy(i, (offset_of(NZ - 1 - i) + NZ) % NZ).start()

    delta_row = jnp.concatenate([delta[xx, 0:1, :] for xx in range(NX)], axis=1)

    def grad(i, store, t):
        j = NZ - 1 - i
        zz = (z + offset_of(j) + NZ) % NZ

        @pl.when(i >= 1)
        def _():
            fold_core(i - 1)

        @pl.when(i >= 2)
        def _():
            send_z(i - 2)

        vc_copy(j).wait_recv()
        keys = k_all[zz].reshape(TILE, HD)
        values = v_all[zz].reshape(TILE, HD)
        queries = q_all[...].reshape(COLS, HD)
        cots = d_all[...].reshape(COLS, HD)
        dprob = dot(values, cots, 1, 1)
        probs = jnp.exp2(store[t] - lse[...])
        dscore = (probs * (dprob - delta_row)).astype(bf16)
        half = probs.astype(bf16)
        dq_acc[...] += dot(keys, dscore, 0, 0)
        own_rows = pl.ds(pl.multiple_of(c * HALF, HALF), HALF)
        gone_rows = pl.ds(pl.multiple_of((1 - c) * HALF, HALF), HALF)
        stage[:, 0:HD] = dot(dscore, queries, 1, 0) * SCALE
        stage[:, HD:2 * HD] = dot(half, cots, 1, 0)
        core_send[i] = stage[gone_rows, :].astype(bf16)
        pc_copy(i).start()
        own[i] = stage[own_rows, :]

    def grad_pair(t, _):
        grad(2 * t, s_odd, NZ // 2 - 1 - t)
        grad(2 * t + 1, s_even, NZ // 2 - 1 - t)
        return 0

    lax.fori_loop(0, NZ // 2, grad_pair, 0)

    for e in range(1, NX):
        cols = pl.ds(pl.multiple_of(((x + e) % NX) * WIDE, WIDE), WIDE)
        dq_send[e - 1] = dq_acc[:, cols].astype(bf16)
        g_copy(e).start()
    fold_core(NZ - 1)
    send_z(NZ - 2)
    kv_sum = fold_y(NZ - 1)

    mine = pl.ds(pl.multiple_of(x * WIDE, WIDE), WIDE)
    dq_sum = dq_acc[:, mine]
    for e in range(1, NX):
        g_copy(e).wait_recv()
        dq_sum = dq_sum + dq_got[e - 1].astype(f32)
    dq_rows = jnp.transpose(dq_sum * SCALE).astype(bf16)
    for h in range(HEADS):
        dq_out[:, h * HD:(h + 1) * HD] = dq_rows[h * ROWS:(h + 1) * ROWS, :]

    for e in range(1, NZ):
        pz_copy(0, e).wait_recv()
        kv_sum = kv_sum + z_got[e - 1].astype(f32)
    dk_out[...] = kv_sum[:, 0:HD].astype(bf16)
    dv_out[...] = kv_sum[:, HD:2 * HD].astype(bf16)

    for e in range(1, NX):
        q_copy(e).wait_send()
        d_copy(e).wait_send()
        e_copy(e).wait_send()
        l_copy(e).wait_send()
        g_copy(e).wait_send()
    for e in range(1, NZ):
        kz_copy(e).wait_send()
        vz_copy(e).wait_send()
        pz_copy(0, e).wait_send()

    def drain(j, _):
        for e in range(1, NY):
            ky_copy(j, e).wait_send()
            vy_copy(j, e).wait_send()
            py_copy(j, e).wait_send()
        kc_copy(j).wait_send()
        vc_copy(j).wait_send()
        pc_copy(j).wait_send()
        return 0

    lax.fori_loop(0, NZ, drain, 0)


def local(queries, key_vecs, value_vecs, outputs, out_grad, positions):
    starts = positions[::ROWS]
    vmem = pl.BlockSpec(memory_space=pltpu.VMEM)
    dma = pltpu.SemaphoreType.DMA
    V = pltpu.VMEM
    return pl.pallas_call(
        kernel,
        out_shape=(
            jax.ShapeDtypeStruct((ROWS, HEADS * HD), bf16),
            jax.ShapeDtypeStruct((ROWS, HD), bf16),
            jax.ShapeDtypeStruct((ROWS, HD), bf16),
        ),
        in_specs=[pl.BlockSpec(memory_space=pltpu.SMEM)] + [vmem] * 5,
        out_specs=(vmem, vmem, vmem),
        scratch_shapes=[
            V((NX, WIDE, HD), bf16), V((NX, WIDE, HD), bf16),
            V((NX, 8, WIDE), f32),
            V((8, 256), f32), V((NX - 1, 8, 256), f32), V((1, COLS), f32),
            V((NZ, NC, NY, ROWS, HD), bf16), V((NZ, NC, NY, ROWS, HD), bf16),
            V((NZ * TILE, HD), jnp.int32), V((8, COLS), jnp.int32),
            V((NZ // 2, TILE, COLS), f32), V((NZ // 2, TILE, COLS), f32),
            V((8, COLS), f32), V((8, COLS), f32),
            V((HD, COLS), f32), V((NX - 1, HD, WIDE), bf16), V((NX - 1, HD, WIDE), bf16),
            V((TILE, 2 * HD), f32),
            V((NZ, HALF, 2 * HD), f32),
            V((NZ, HALF, 2 * HD), bf16), V((NZ, HALF, 2 * HD), bf16),
            V((NZ, NY, ROWS, 2 * HD), bf16), V((NZ, NY - 1, ROWS, 2 * HD), bf16),
            V((NZ, ROWS, 2 * HD), bf16), V((NZ - 1, ROWS, 2 * HD), bf16),
        ]
        + [dma((NX - 1,))] * 10
        + [dma((NZ - 1,)), dma((NZ - 1,)), dma((NZ, NY - 1)), dma((NZ, NY - 1)), dma((NZ,)), dma((NZ,))] * 2
        + [dma((NZ,)), dma((NZ,)), dma((NZ, NY - 1)), dma((NZ, NY - 1)), dma((NZ - 1,)), dma((NZ - 1,))],
        compiler_params=pltpu.CompilerParams(
            collective_id=0, has_side_effects=True, vmem_limit_bytes=62 * 2**20
        ),
        cost_estimate=pl.CostEstimate(
            flops=12 * COLS * NZ * TILE * HD, bytes_accessed=1 << 20, transcendentals=2 * COLS * NZ * TILE
        ),
    )(starts, queries, key_vecs, value_vecs, outputs, out_grad)


def solution(mesh):
    rows = P(("pb", "ka"), None)
    return jax.shard_map(
        local,
        mesh=mesh,
        in_specs=(rows, rows, rows, rows, rows, P()),
        out_specs=(rows, rows, rows),
        check_vma=False,
    )
```

```python
import math

import jax
import jax.numpy as jnp
from jax import lax
from jax.experimental import pallas as pl
from jax.experimental.pallas import tpu as pltpu
from jax.sharding import PartitionSpec as P

HEADS = 8
HD = 128
NX, NY, NZ, NC = 4, 4, 8, 2
ROWS = 64
WIDE = HEADS * ROWS
COLS = NX * WIDE
PART = WIDE // 2
SIDE = COLS // 2
TILE = NC * NY * ROWS
AHEAD = 3
HALF = NY * ROWS

HIDDEN = -1e30
FLOOR = -1e20
SCALE = HD ** -0.5
LOG2E = math.log2(math.e)

f32 = jnp.float32
bf16 = jnp.bfloat16
MESH = pl.DeviceIdType.MESH


def dot(left, right, cl, cr):
    return lax.dot_general(
        left, right, (((cl,), (cr,)), ((), ())), preferred_element_type=f32
    )


def where_is(x, y, z, c):
    return {"pb": y * 4 + z // 2, "ka": (z % 2) * 8 + x * 2 + c}


def offset_of(j):
    return ((j + 1) // 2) * (2 * (j % 2) - 1)


def kernel(
    p_hbm, q_hbm, k_hbm, v_hbm, o_hbm, d_hbm,
    dq_hbm, dk_hbm, dv_hbm,
    p_in, q_in, o_in, d_in, dq_out, dk_out, dv_out, ios,
    q_all, d_all, delta, lse_own, lse_got, lse,
    k_all, v_all, k_mask, q_mask,
    s_even, s_odd, top, total,
    dq_acc, dq_send, dq_got, stage, stage2,
    own, core_send, core_got, y_send, y_got, z_send, z_got,
    qs, qr, ds, dr, es, er, ls, lr, gs, gr,
    kzs, kzr, kys, kyr, kcs, kcr,
    vzs, vzr, vys, vyr, vcs, vcr,
    pcs, pcr, pys, pyr, pzs, pzr,
):
    pb, ka = lax.axis_index("pb"), lax.axis_index("ka")
    y = pb // 4
    z = (pb % 4) * 2 + ka // 8
    x = (ka // 2) % 4
    c = ka % 2

    def send(src, dst, ssem, rsem, to):
        return pltpu.make_async_remote_copy(
            src_ref=src, dst_ref=dst, send_sem=ssem, recv_sem=rsem,
            device_id=to, device_id_type=MESH,
        )

    core_peer = where_is(x, y, z, 1 - c)

    def x_peer(e):
        return where_is((x + e) % NX, y, z, c)

    def y_peer(e):
        return where_is(x, (y + e) % NY, z, c)

    def z_peer(e):
        return where_is(x, y, (z + e) % NZ, c)

    barrier = pltpu.get_barrier_semaphore()
    peers = [core_peer]
    peers += [x_peer(e) for e in range(1, NX)]
    peers += [y_peer(e) for e in range(1, NY)]
    peers += [z_peer(e) for e in range(1, NZ)]
    for peer in peers:
        pl.semaphore_signal(barrier, inc=1, device_id=peer, device_id_type=MESH)

    loads = [
        pltpu.make_async_copy(src, dst, ios.at[n])
        for n, (src, dst) in enumerate((
            (q_hbm, q_in), (k_hbm, k_all.at[z, c, y]), (d_hbm, d_in),
            (v_hbm, v_all.at[z, c, y]), (o_hbm, o_in), (p_hbm, p_in),
        ))
    ]
    for load in loads:
        load.start()
    for load in loads:
        load.wait()
    q = q_in[...]
    d = d_in[...]
    for h in range(HEADS):
        rows = pl.ds((h % 4) * ROWS, ROWS)
        q_all[h // 4, x, rows, :] = q[:, h * HD:(h + 1) * HD]
        d_all[h // 4, x, rows, :] = d[:, h * HD:(h + 1) * HD]

    pl.semaphore_wait(barrier, len(peers))

    def q_copy(side, e):
        part = q_all.at[side, x]
        return send(part, part, qs.at[side, e - 1], qr.at[side, e - 1], x_peer(e))

    def d_copy(e):
        part = d_all.at[:, x]
        return send(part, part, ds.at[e - 1], dr.at[e - 1], x_peer(e))

    def e_copy(e):
        return send(delta.at[x], delta.at[x], es.at[e - 1], er.at[e - 1], x_peer(e))

    def l_copy(side, e):
        return send(
            lse_own.at[side], lse_got.at[side, e - 1],
            ls.at[side, e - 1], lr.at[side, e - 1], x_peer(e),
        )

    def g_copy(e):
        return send(dq_send.at[e - 1], dq_got.at[e - 1], gs.at[e - 1], gr.at[e - 1], x_peer(e))

    def kz_copy(e):
        own_k = k_all.at[z, c, y]
        return send(own_k, own_k, kzs.at[e - 1], kzr.at[e - 1], z_peer(e))

    def vz_copy(e):
        own_v = v_all.at[z, c, y]
        return send(own_v, own_v, vzs.at[e - 1], vzr.at[e - 1], z_peer(e))

    def ky_copy(j, e):
        part = k_all.at[(z + offset_of(j) + NZ) % NZ, c, y]
        return send(part, part, kys.at[j, e - 1], kyr.at[j, e - 1], y_peer(e))

    def vy_copy(j, e):
        part = v_all.at[(z + offset_of(j) + NZ) % NZ, c, y]
        return send(part, part, vys.at[j, e - 1], vyr.at[j, e - 1], y_peer(e))

    def kc_copy(j):
        part = k_all.at[(z + offset_of(j) + NZ) % NZ, c]
        return send(part, part, kcs.at[j], kcr.at[j], core_peer)

    def vc_copy(j):
        part = v_all.at[(z + offset_of(j) + NZ) % NZ, c]
        return send(part, part, vcs.at[j], vcr.at[j], core_peer)

    for e in range(1, NX):
        q_copy(0, e).start()
    for e in (1, 7, 2, 6, 3, 5, 4):
        kz_copy(e).start()
    for e in range(1, NY):
        ky_copy(0, e).start()
    for e in range(1, NX):
        q_copy(1, e).start()

    o = o_in[...].astype(f32) * d.astype(f32)
    prod = jnp.concatenate([o[:, h * HD:(h + 1) * HD] for h in range(HEADS)], axis=0)
    high = prod.astype(bf16)
    low = (prod - high.astype(f32)).astype(bf16)
    ones = jnp.ones((8, HD), bf16)
    delta[x] = dot(ones, high, 1, 1) + dot(ones, low, 1, 1)

    row = lax.broadcasted_iota(jnp.int32, (ROWS, HD), 0)
    lane = lax.broadcasted_iota(jnp.int32, (ROWS, HD), 1)

    def start(xx, yy, zz):
        block = (yy * 4 + zz // 2) * 8 + (zz % 2) * 4 + xx
        return p_in[pl.ds(block, 1), 0:1]

    limit = jnp.full((ROWS, HD), 2 ** 30, jnp.int32)
    for xx in range(NX):
        limit = jnp.where(lane == ROWS + xx, start(xx, y, z), limit)

    def mask_keys(n, _):
        j, cc, yy = n // (NC * NY), (n // NY) % NC, n % NY
        zz = (z + offset_of(j) + NZ) % NZ
        at = pl.ds(pl.multiple_of(n * ROWS, ROWS), ROWS)
        k_mask[at, :] = jnp.where(start(x, yy, zz) > limit, HIDDEN, 0.0).astype(bf16)
        return 0

    lax.fori_loop(0, NZ * NC * NY, mask_keys, 0)
    for cc in range(NC):
        at = pl.ds(pl.multiple_of((cc * NY + y) * ROWS, ROWS), ROWS)
        later = (lane < ROWS) & (row + cc * ROWS > lane + c * ROWS)
        k_mask[at, :] = jnp.where(
            later | (start(x, y, z) > limit), HIDDEN, 0.0
        ).astype(bf16)
    for side in range(2):
        for xx in range(NX):
            mine = (lane == ROWS + xx) | ((lane == row) & (x == xx))
            one = jnp.where(mine, 1.0, 0.0).astype(bf16)
            for h in range(4):
                q_mask[pl.ds(side * SIDE + xx * PART + h * ROWS, ROWS), :] = one

    top[...] = jnp.full_like(top, FLOOR)
    total[...] = jnp.zeros_like(total)
    dq_acc[...] = jnp.zeros_like(dq_acc)

    def forward_keys(j, _):
        arrived = (NZ - offset_of(j)) % NZ
        kz_copy(arrived).wait_recv()
        for e in range(1, NY):
            ky_copy(j, e).start()
        return 0

    def share_keys(j):
        for e in range(1, NY):
            ky_copy(j, e).wait_recv()
        kc_copy(j).start()

    lax.fori_loop(1, 3, forward_keys, 0)
    share_keys(0)
    lax.fori_loop(3, 5, forward_keys, 0)
    share_keys(1)
    lax.fori_loop(5, NZ, forward_keys, 0)
    for e in (1, 7, 2, 6, 3, 5, 4):
        vz_copy(e).start()
    for j in range(2, AHEAD):
        share_keys(j)
    for e in range(1, NX):
        q_copy(0, e).wait_recv()

    def forward_values(j):
        @pl.when(j > 0)
        def _():
            vz_copy((NZ - offset_of(j)) % NZ).wait_recv()

        for e in range(1, NY):
            vy_copy(j, e).start()

    def arrive(j):
        @pl.when(j < NZ - AHEAD)
        def _():
            share_keys(j + AHEAD)

        kc_copy(j).wait_recv()

    def statistics(side, prepare):
        cols = pl.ds(side * SIDE, SIDE)
        queries = jnp.concatenate(
            [q_all[side].reshape(SIDE, HD), q_mask[cols, :]], axis=1
        )

        def scores(j, store, t):
            zz = (z + offset_of(j) + NZ) % NZ
            at = pl.ds(pl.multiple_of(j * TILE, TILE), TILE)
            keys = jnp.concatenate([k_all[zz].reshape(TILE, HD), k_mask[at, :]], axis=1)
            raw = dot(keys, queries, 1, 1) * (SCALE * LOG2E)
            store[t, :, cols] = raw
            return jnp.max(raw.reshape(TILE // 8, 8, SIDE), axis=0)

        def sums(store, t, high):
            part = store[t, :, cols].reshape(TILE // 8, 8, SIDE)
            return jnp.sum(jnp.exp2(part - high[None]), axis=0)

        def step(j, store, t, before, s):
            prepare(j)
            high = top[:, cols]
            seen = scores(j, store, t)
            run = total[:, cols] + sums(before, s, high)
            new = jnp.maximum(high, seen)
            total[:, cols] = run * jnp.exp2(high - new)
            top[:, cols] = new

        prepare(jnp.int32(0))
        top[:, cols] = jnp.maximum(top[:, cols], scores(0, s_even, 0))

        def pair(t, _):
            step(2 * t + 1, s_odd, t, s_even, t)

            @pl.when(t < NZ // 2 - 1)
            def _():
                step(2 * t + 2, s_even, t + 1, s_odd, t)

            return 0

        lax.fori_loop(0, NZ // 2, pair, 0)
        high = top[:, cols]
        run = total[:, cols] + sums(s_odd, NZ // 2 - 1, high)
        peak = jnp.max(high, axis=0, keepdims=True)
        mass = jnp.sum(run * jnp.exp2(high - peak), axis=0, keepdims=True)
        mine = jnp.where(mass > 0.0, peak + jnp.log2(mass), FLOOR)
        for n in range(8):
            lse_own[side, n:n + 1, :] = mine[:, n * HD:(n + 1) * HD]
        for e in range(1, NX):
            l_copy(side, e).start()

    def join(side):
        for e in range(1, NX):
            l_copy(side, e).wait_recv()
        parts = [lse_own[side]] + [lse_got[side, e] for e in range(NX - 1)]
        peak = jnp.maximum(jnp.maximum(parts[0], parts[1]), jnp.maximum(parts[2], parts[3]))
        joint = peak + jnp.log2(sum(jnp.exp2(part - peak) for part in parts))
        for n in range(8):
            lse[:, side * SIDE + n * HD:side * SIDE + (n + 1) * HD] = joint[n:n + 1, :]

    statistics(0, arrive)
    for e in range(1, NX):
        q_copy(1, e).wait_recv()
    for e in range(1, NX):
        d_copy(e).start()
        e_copy(e).start()
    statistics(1, forward_values)

    def share_values(j, _):
        for e in range(1, NY):
            vy_copy(j, e).wait_recv()
        vc_copy(j).start()
        return 0

    lax.fori_loop(0, NZ, share_values, 0)
    for e in range(1, NX):
        d_copy(e).wait_recv()
        e_copy(e).wait_recv()
    join(0)

    def pc_copy(i):
        return send(core_send.at[i], core_got.at[i], pcs.at[i], pcr.at[i], core_peer)

    def py_copy(i, e):
        return send(
            y_send.at[i, (y + e) % NY], y_got.at[i, e - 1],
            pys.at[i, e - 1], pyr.at[i, e - 1], y_peer(e),
        )

    def pz_copy(i, e):
        return send(z_send.at[i], z_got.at[e - 1], pzs.at[e - 1], pzr.at[e - 1], z_peer(e))

    def fold_core(i):
        pc_copy(i).wait_recv()
        both = own[i] + core_got[i].astype(f32)
        y_send[i] = both.astype(bf16).reshape(NY, ROWS, 2 * HD)
        for e in range(1, NY):
            py_copy(i, e).start()

    def fold_y(i):
        for e in range(1, NY):
            py_copy(i, e).wait_recv()
        part = y_send[i, y].astype(f32)
        for e in range(NY - 1):
            part = part + y_got[i, e].astype(f32)
        return part

    def send_z(i):
        z_send[i] = fold_y(i).astype(bf16)
        pz_copy(i, (offset_of(NZ - 1 - i) + NZ) % NZ).start()

    def delta_of(side):
        cols = slice(side * PART, (side + 1) * PART)
        return jnp.concatenate([delta[xx, 0:1, cols] for xx in range(NX)], axis=1)


    def ready(i):
        j = NZ - 1 - i
        zz = (z + offset_of(j) + NZ) % NZ

        @pl.when(i >= 2)
        def _():
            fold_core(i - 2)

        @pl.when(i >= 3)
        def _():
            send_z(i - 3)

        vc_copy(j).wait_recv()
        keys = k_all[zz].reshape(TILE, HD)
        values = v_all[zz].reshape(TILE, HD)
        return keys, values

    def terms(keys, values, queries, cots, scored, norm, drop):
        dprob = dot(values, cots, 1, 1)
        probs = jnp.exp2(scored - norm)
        dscore = (probs * (dprob - drop)).astype(bf16)
        half = probs.astype(bf16)
        dv = dot(half, cots, 1, 0)
        dk = dot(dscore, queries, 1, 0)
        return dot(keys, dscore, 0, 0), dk, dv

    def hand_over(i, stage):
        own_rows = pl.ds(pl.multiple_of(c * HALF, HALF), HALF)
        gone_rows = pl.ds(pl.multiple_of((1 - c) * HALF, HALF), HALF)
        core_send[i] = stage[gone_rows, :].astype(bf16)
        pc_copy(i).start()
        own[i] = stage[own_rows, :]

    def grad_side(side, keys, values, store, t, stage):
        cols = pl.ds(side * SIDE, SIDE)
        dq, dk, dv = terms(
            keys, values, q_all[side].reshape(SIDE, HD), d_all[side].reshape(SIDE, HD),
            store[t, :, cols], lse[:, cols], delta_of(side),
        )
        dq_acc[:, cols] += dq
        if side == 0:
            stage[:, 0:HD] = dk * SCALE
            stage[:, HD:2 * HD] = dv
        else:
            stage[:, 0:HD] += dk * SCALE
            stage[:, HD:2 * HD] += dv

    def grad(i, store, t):
        keys, values = ready(i)
        dq, dk, dv = terms(
            keys, values, q_all[...].reshape(COLS, HD), d_all[...].reshape(COLS, HD),
            store[t], lse[...], jnp.concatenate([delta_of(0), delta_of(1)], axis=1),
        )
        dq_acc[...] += dq
        stage[:, 0:HD] = dk * SCALE
        stage[:, HD:2 * HD] = dv
        hand_over(i, stage)

    first, second = ready(0), ready(1)
    grad_side(0, *first, s_odd, NZ // 2 - 1, stage)
    grad_side(0, *second, s_even, NZ // 2 - 1, stage2)
    join(1)
    grad_side(1, *first, s_odd, NZ // 2 - 1, stage)
    hand_over(0, stage)
    grad_side(1, *second, s_even, NZ // 2 - 1, stage2)
    hand_over(1, stage2)

    def grad_pair(t, _):
        grad(2 * t, s_odd, NZ // 2 - 1 - t)

        @pl.when(t < NZ // 2 - 1)
        def _():
            grad(2 * t + 1, s_even, NZ // 2 - 1 - t)

        return 0

    lax.fori_loop(1, NZ // 2, grad_pair, 0)

    keys, values = ready(NZ - 1)

    def last(e, fresh):
        xx = (x + e) % NX
        spans = [
            pl.ds(pl.multiple_of(side * SIDE + xx * PART, PART), PART) for side in range(2)
        ]

        def both(pick, axis):
            return jnp.concatenate([pick(side) for side in range(2)], axis=axis)

        dq, dk, dv = terms(
            keys, values,
            both(lambda side: q_all[side, xx], 0), both(lambda side: d_all[side, xx], 0),
            both(lambda side: s_even[0, :, spans[side]], 1),
            both(lambda side: lse[:, spans[side]], 1), delta[xx, 0:1, :],
        )
        if fresh:
            stage[:, 0:HD] = dk * SCALE
            stage[:, HD:2 * HD] = dv
        else:
            stage[:, 0:HD] += dk * SCALE
            stage[:, HD:2 * HD] += dv
        return both(lambda side: dq_acc[:, spans[side]], 1) + dq

    for e in (2, 1, 3):
        dq_send[e - 1] = last(e, e == 2).astype(bf16)
        g_copy(e).start()
    fold_core(NZ - 2)
    send_z(NZ - 3)
    dq_sum = last(0, False)
    hand_over(NZ - 1, stage)

    fold_core(NZ - 1)
    send_z(NZ - 2)

    for e in range(1, NX):
        g_copy(e).wait_recv()
        dq_sum = dq_sum + dq_got[e - 1].astype(f32)
    dq_rows = jnp.transpose(dq_sum * SCALE).astype(bf16)
    for h in range(HEADS):
        dq_out[:, h * HD:(h + 1) * HD] = dq_rows[h * ROWS:(h + 1) * ROWS, :]

    dq_store = pltpu.make_async_copy(dq_out, dq_hbm, ios.at[0])
    dq_store.start()
    kv_sum = fold_y(NZ - 1)
    for e in range(1, NZ):
        pz_copy(0, e).wait_recv()
        kv_sum = kv_sum + z_got[e - 1].astype(f32)
    dk_out[...] = kv_sum[:, 0:HD].astype(bf16)
    dv_out[...] = kv_sum[:, HD:2 * HD].astype(bf16)
    dk_store = pltpu.make_async_copy(dk_out, dk_hbm, ios.at[1])
    dv_store = pltpu.make_async_copy(dv_out, dv_hbm, ios.at[2])
    dk_store.start()
    dv_store.start()

    for e in range(1, NX):
        q_copy(0, e).wait_send()
        q_copy(1, e).wait_send()
        d_copy(e).wait_send()
        e_copy(e).wait_send()
        l_copy(0, e).wait_send()
        l_copy(1, e).wait_send()
        g_copy(e).wait_send()
    for e in range(1, NZ):
        kz_copy(e).wait_send()
        vz_copy(e).wait_send()
        pz_copy(0, e).wait_send()

    def drain(j, _):
        for e in range(1, NY):
            ky_copy(j, e).wait_send()
            vy_copy(j, e).wait_send()
            py_copy(j, e).wait_send()
        kc_copy(j).wait_send()
        vc_copy(j).wait_send()
        pc_copy(j).wait_send()
        return 0

    lax.fori_loop(0, NZ, drain, 0)
    dq_store.wait()
    dk_store.wait()
    dv_store.wait()


def local(queries, key_vecs, value_vecs, outputs, out_grad, positions):
    blocks = positions.reshape(-1, NC * ROWS)
    hbm = pl.BlockSpec(memory_space=pl.ANY)
    dma = pltpu.SemaphoreType.DMA
    V = pltpu.VMEM
    return pl.pallas_call(
        kernel,
        out_shape=(
            jax.ShapeDtypeStruct((ROWS, HEADS * HD), bf16),
            jax.ShapeDtypeStruct((ROWS, HD), bf16),
            jax.ShapeDtypeStruct((ROWS, HD), bf16),
        ),
        in_specs=[hbm] * 6,
        out_specs=(hbm, hbm, hbm),
        scratch_shapes=[
            V((NX * NY * NZ, NC * ROWS), jnp.int32),
            V((ROWS, HEADS * HD), bf16), V((ROWS, HEADS * HD), bf16), V((ROWS, HEADS * HD), bf16),
            V((ROWS, HEADS * HD), bf16), V((ROWS, HD), bf16), V((ROWS, HD), bf16), dma((6,)),
            V((2, NX, PART, HD), bf16), V((2, NX, PART, HD), bf16),
            V((NX, 8, WIDE), f32),
            V((2, 8, HD), f32), V((2, NX - 1, 8, HD), f32), V((1, COLS), f32),
            V((NZ, NC, NY, ROWS, HD), bf16), V((NZ, NC, NY, ROWS, HD), bf16),
            V((NZ * TILE, HD), bf16), V((COLS, HD), bf16),
            V((NZ // 2, TILE, COLS), f32), V((NZ // 2, TILE, COLS), f32),
            V((8, COLS), f32), V((8, COLS), f32),
            V((HD, COLS), f32), V((NX - 1, HD, WIDE), bf16), V((NX - 1, HD, WIDE), bf16),
            V((TILE, 2 * HD), f32), V((TILE, 2 * HD), f32),
            V((NZ, HALF, 2 * HD), f32),
            V((NZ, HALF, 2 * HD), bf16), V((NZ, HALF, 2 * HD), bf16),
            V((NZ, NY, ROWS, 2 * HD), bf16), V((NZ, NY - 1, ROWS, 2 * HD), bf16),
            V((NZ, ROWS, 2 * HD), bf16), V((NZ - 1, ROWS, 2 * HD), bf16),
        ]
        + [dma((2, NX - 1))] * 2 + [dma((NX - 1,))] * 4 + [dma((2, NX - 1))] * 2 + [dma((NX - 1,))] * 2
        + [dma((NZ - 1,)), dma((NZ - 1,)), dma((NZ, NY - 1)), dma((NZ, NY - 1)), dma((NZ,)), dma((NZ,))] * 2
        + [dma((NZ,)), dma((NZ,)), dma((NZ, NY - 1)), dma((NZ, NY - 1)), dma((NZ - 1,)), dma((NZ - 1,))],
        compiler_params=pltpu.CompilerParams(
            collective_id=0, has_side_effects=True, vmem_limit_bytes=62 * 2**20
        ),
        cost_estimate=pl.CostEstimate(
            flops=12 * COLS * NZ * TILE * HD, bytes_accessed=1 << 20, transcendentals=2 * COLS * NZ * TILE
        ),
    )(blocks, queries, key_vecs, value_vecs, outputs, out_grad)


def solution(mesh):
    rows = P(("pb", "ka"), None)
    return jax.shard_map(
        local,
        mesh=mesh,
        in_specs=(rows, rows, rows, rows, rows, P()),
        out_specs=(rows, rows, rows),
        check_vma=False,
    )
```

```python
import math

import jax
import jax.numpy as jnp
from jax import lax
from jax.experimental import pallas as pl
from jax.experimental.pallas import tpu as pltpu
from jax.sharding import PartitionSpec as P

HEADS = 8
HD = 128
NX, NY, NZ, NC = 4, 4, 8, 2
ROWS = 64
WIDE = HEADS * ROWS
COLS = NX * WIDE
PART = WIDE // 2
SIDE = COLS // 2
TILE = NC * NY * ROWS
AHEAD = 3
HALF = NY * ROWS

HIDDEN = -1e30
FLOOR = -1e20
SCALE = HD ** -0.5
LOG2E = math.log2(math.e)

f32 = jnp.float32
bf16 = jnp.bfloat16
MESH = pl.DeviceIdType.MESH


def dot(left, right, cl, cr):
    return lax.dot_general(
        left, right, (((cl,), (cr,)), ((), ())), preferred_element_type=f32
    )


def where_is(x, y, z, c):
    return {"pb": y * 4 + z // 2, "ka": (z % 2) * 8 + x * 2 + c}


def offset_of(j):
    return ((j + 1) // 2) * (2 * (j % 2) - 1)


def kernel(
    p_hbm, q_hbm, k_hbm, v_hbm, o_hbm, d_hbm,
    dq_hbm, dk_hbm, dv_hbm,
    p_in, q_in, o_in, d_in, dq_out, dk_out, dv_out, ios,
    q_all, d_all, delta, lse_own, lse_got, lse,
    k_all, v_all, k_mask, q_mask,
    s_even, s_odd, top, total,
    dq_acc, dq_send, dq_got, stage, stage2,
    own, core_send, core_got, y_send, y_got, z_send, z_got,
    qs, qr, ds, dr, es, er, ls, lr, gs, gr,
    kzs, kzr, kys, kyr, kcs, kcr,
    vzs, vzr, vys, vyr, vcs, vcr,
    pcs, pcr, pys, pyr, pzs, pzr,
):
    pb, ka = lax.axis_index("pb"), lax.axis_index("ka")
    y = pb // 4
    z = (pb % 4) * 2 + ka // 8
    x = (ka // 2) % 4
    c = ka % 2

    def send(src, dst, ssem, rsem, to):
        return pltpu.make_async_remote_copy(
            src_ref=src, dst_ref=dst, send_sem=ssem, recv_sem=rsem,
            device_id=to, device_id_type=MESH,
        )

    core_peer = where_is(x, y, z, 1 - c)

    def x_peer(e):
        return where_is((x + e) % NX, y, z, c)

    def y_peer(e):
        return where_is(x, (y + e) % NY, z, c)

    def z_peer(e):
        return where_is(x, y, (z + e) % NZ, c)

    barrier = pltpu.get_barrier_semaphore()
    peers = [core_peer]
    peers += [x_peer(e) for e in range(1, NX)]
    peers += [y_peer(e) for e in range(1, NY)]
    peers += [z_peer(e) for e in range(1, NZ)]
    for peer in peers:
        pl.semaphore_signal(barrier, inc=1, device_id=peer, device_id_type=MESH)

    loads = [
        pltpu.make_async_copy(src, dst, ios.at[n])
        for n, (src, dst) in enumerate((
            (q_hbm, q_in), (k_hbm, k_all.at[z, c, y]), (d_hbm, d_in),
            (v_hbm, v_all.at[z, c, y]), (o_hbm, o_in), (p_hbm, p_in),
        ))
    ]
    for load in loads:
        load.start()
    for load in loads:
        load.wait()
    q = q_in[...]
    d = d_in[...]
    for h in range(HEADS):
        rows = pl.ds((h % 4) * ROWS, ROWS)
        q_all[h // 4, x, rows, :] = q[:, h * HD:(h + 1) * HD]
        d_all[h // 4, x, rows, :] = d[:, h * HD:(h + 1) * HD]

    pl.semaphore_wait(barrier, len(peers))

    def q_copy(side, e):
        part = q_all.at[side, x]
        return send(part, part, qs.at[side, e - 1], qr.at[side, e - 1], x_peer(e))

    def d_copy(e):
        part = d_all.at[:, x]
        return send(part, part, ds.at[e - 1], dr.at[e - 1], x_peer(e))

    def e_copy(e):
        return send(delta.at[x], delta.at[x], es.at[e - 1], er.at[e - 1], x_peer(e))

    def l_copy(side, e):
        return send(
            lse_own.at[side], lse_got.at[side, e - 1],
            ls.at[side, e - 1], lr.at[side, e - 1], x_peer(e),
        )

    def g_copy(e):
        return send(dq_send.at[e - 1], dq_got.at[e - 1], gs.at[e - 1], gr.at[e - 1], x_peer(e))

    def kz_copy(e):
        own_k = k_all.at[z, c, y]
        return send(own_k, own_k, kzs.at[e - 1], kzr.at[e - 1], z_peer(e))

    def vz_copy(e):
        own_v = v_all.at[z, c, y]
        return send(own_v, own_v, vzs.at[e - 1], vzr.at[e - 1], z_peer(e))

    def ky_copy(j, e):
        part = k_all.at[(z + offset_of(j) + NZ) % NZ, c, y]
        return send(part, part, kys.at[j, e - 1], kyr.at[j, e - 1], y_peer(e))

    def vy_copy(j, e):
        part = v_all.at[(z + offset_of(j) + NZ) % NZ, c, y]
        return send(part, part, vys.at[j, e - 1], vyr.at[j, e - 1], y_peer(e))

    def kc_copy(j):
        part = k_all.at[(z + offset_of(j) + NZ) % NZ, c]
        return send(part, part, kcs.at[j], kcr.at[j], core_peer)

    def vc_copy(j):
        part = v_all.at[(z + offset_of(j) + NZ) % NZ, c]
        return send(part, part, vcs.at[j], vcr.at[j], core_peer)

    for e in range(1, NX):
        q_copy(0, e).start()
    for e in (1, 7, 2, 6, 3, 5, 4):
        kz_copy(e).start()
    for e in range(1, NY):
        ky_copy(0, e).start()
    for e in range(1, NX):
        q_copy(1, e).start()
    for e in range(1, NX):
        d_copy(e).start()

    o = o_in[...].astype(f32) * d.astype(f32)
    prod = jnp.concatenate([o[:, h * HD:(h + 1) * HD] for h in range(HEADS)], axis=0)
    high = prod.astype(bf16)
    low = (prod - high.astype(f32)).astype(bf16)
    ones = jnp.ones((8, HD), bf16)
    delta[x] = dot(ones, high, 1, 1) + dot(ones, low, 1, 1)
    for e in range(1, NX):
        e_copy(e).start()

    row = lax.broadcasted_iota(jnp.int32, (ROWS, HD), 0)
    lane = lax.broadcasted_iota(jnp.int32, (ROWS, HD), 1)

    def start(xx, yy, zz):
        block = (yy * 4 + zz // 2) * 8 + (zz % 2) * 4 + xx
        return p_in[pl.ds(block, 1), 0:1]

    limit = jnp.full((ROWS, HD), 2 ** 30, jnp.int32)
    for xx in range(NX):
        limit = jnp.where(lane == ROWS + xx, start(xx, y, z), limit)

    def mask_keys(n, _):
        j, cc, yy = n // (NC * NY), (n // NY) % NC, n % NY
        zz = (z + offset_of(j) + NZ) % NZ
        at = pl.ds(pl.multiple_of(n * ROWS, ROWS), ROWS)
        k_mask[at, :] = jnp.where(start(x, yy, zz) > limit, HIDDEN, 0.0).astype(bf16)
        return 0

    lax.fori_loop(0, NZ * NC * NY, mask_keys, 0)
    for cc in range(NC):
        at = pl.ds(pl.multiple_of((cc * NY + y) * ROWS, ROWS), ROWS)
        later = (lane < ROWS) & (row + cc * ROWS > lane + c * ROWS)
        k_mask[at, :] = jnp.where(
            later | (start(x, y, z) > limit), HIDDEN, 0.0
        ).astype(bf16)
    for side in range(2):
        for xx in range(NX):
            mine = (lane == ROWS + xx) | ((lane == row) & (x == xx))
            one = jnp.where(mine, 1.0, 0.0).astype(bf16)
            for h in range(4):
                q_mask[pl.ds(side * SIDE + xx * PART + h * ROWS, ROWS), :] = one

    top[...] = jnp.full_like(top, FLOOR)
    total[...] = jnp.zeros_like(total)
    dq_acc[...] = jnp.zeros_like(dq_acc)

    def forward_keys(j, _):
        arrived = (NZ - offset_of(j)) % NZ
        kz_copy(arrived).wait_recv()
        for e in range(1, NY):
            ky_copy(j, e).start()
        return 0

    def share_keys(j):
        for e in range(1, NY):
            ky_copy(j, e).wait_recv()
        kc_copy(j).start()

    lax.fori_loop(1, 3, forward_keys, 0)
    share_keys(0)
    lax.fori_loop(3, 5, forward_keys, 0)
    share_keys(1)
    lax.fori_loop(5, NZ, forward_keys, 0)
    for e in (1, 7, 2, 6, 3, 5, 4):
        vz_copy(e).start()
    for j in range(2, AHEAD):
        share_keys(j)
    for e in range(1, NX):
        q_copy(0, e).wait_recv()

    def forward_values(j):
        @pl.when(j > 0)
        def _():
            vz_copy((NZ - offset_of(j)) % NZ).wait_recv()

        for e in range(1, NY):
            vy_copy(j, e).start()

    def share_values(j):
        for e in range(1, NY):
            vy_copy(NZ - 1 - j, e).wait_recv()
        vc_copy(NZ - 1 - j).start()

    def arrive(j):
        @pl.when(j < NZ - AHEAD)
        def _():
            share_keys(j + AHEAD)

        @pl.when(j >= NZ // 2)
        def _():
            forward_values(2 * NZ - 1 - 2 * j)
            forward_values(2 * NZ - 2 - 2 * j)

        kc_copy(j).wait_recv()

    def statistics(side, prepare):
        cols = pl.ds(side * SIDE, SIDE)
        queries = jnp.concatenate(
            [q_all[side].reshape(SIDE, HD), q_mask[cols, :]], axis=1
        )

        def scores(j, store, t):
            zz = (z + offset_of(j) + NZ) % NZ
            at = pl.ds(pl.multiple_of(j * TILE, TILE), TILE)
            keys = jnp.concatenate([k_all[zz].reshape(TILE, HD), k_mask[at, :]], axis=1)
            raw = dot(keys, queries, 1, 1) * (SCALE * LOG2E)
            store[t, :, cols] = raw
            return jnp.max(raw.reshape(TILE // 8, 8, SIDE), axis=0)

        def sums(store, t, high):
            part = store[t, :, cols].reshape(TILE // 8, 8, SIDE)
            return jnp.sum(jnp.exp2(part - high[None]), axis=0)

        def step(j, store, t, before, s):
            prepare(j)
            high = top[:, cols]
            seen = scores(j, store, t)
            run = total[:, cols] + sums(before, s, high)
            new = jnp.maximum(high, seen)
            total[:, cols] = run * jnp.exp2(high - new)
            top[:, cols] = new

        prepare(jnp.int32(0))
        top[:, cols] = jnp.maximum(top[:, cols], scores(0, s_even, 0))

        def pair(t, _):
            step(2 * t + 1, s_odd, t, s_even, t)

            @pl.when(t < NZ // 2 - 1)
            def _():
                step(2 * t + 2, s_even, t + 1, s_odd, t)

            return 0

        lax.fori_loop(0, NZ // 2, pair, 0)
        high = top[:, cols]
        run = total[:, cols] + sums(s_odd, NZ // 2 - 1, high)
        peak = jnp.max(high, axis=0, keepdims=True)
        mass = jnp.sum(run * jnp.exp2(high - peak), axis=0, keepdims=True)
        mine = jnp.where(mass > 0.0, peak + jnp.log2(mass), FLOOR)
        for n in range(8):
            lse_own[side, n:n + 1, :] = mine[:, n * HD:(n + 1) * HD]
        for e in range(1, NX):
            l_copy(side, e).start()

    def join(side):
        for e in range(1, NX):
            l_copy(side, e).wait_recv()
        parts = [lse_own[side]] + [lse_got[side, e] for e in range(NX - 1)]
        peak = jnp.maximum(jnp.maximum(parts[0], parts[1]), jnp.maximum(parts[2], parts[3]))
        joint = peak + jnp.log2(sum(jnp.exp2(part - peak) for part in parts))
        for n in range(8):
            lse[:, side * SIDE + n * HD:side * SIDE + (n + 1) * HD] = joint[n:n + 1, :]

    statistics(0, arrive)
    for e in range(1, NX):
        q_copy(1, e).wait_recv()
    statistics(1, share_values)

    for e in range(1, NX):
        d_copy(e).wait_recv()
        e_copy(e).wait_recv()
    join(0)

    def pc_copy(i):
        return send(core_send.at[i], core_got.at[i], pcs.at[i], pcr.at[i], core_peer)

    def py_copy(i, e):
        return send(
            y_send.at[i, (y + e) % NY], y_got.at[i, e - 1],
            pys.at[i, e - 1], pyr.at[i, e - 1], y_peer(e),
        )

    def pz_copy(i, e):
        return send(z_send.at[i], z_got.at[e - 1], pzs.at[e - 1], pzr.at[e - 1], z_peer(e))

    def fold_core(i):
        pc_copy(i).wait_recv()
        both = own[i] + core_got[i].astype(f32)
        y_send[i] = both.astype(bf16).reshape(NY, ROWS, 2 * HD)
        for e in range(1, NY):
            py_copy(i, e).start()

    def fold_y(i):
        for e in range(1, NY):
            py_copy(i, e).wait_recv()
        part = y_send[i, y].astype(f32)
        for e in range(NY - 1):
            part = part + y_got[i, e].astype(f32)
        return part

    def send_z(i):
        z_send[i] = fold_y(i).astype(bf16)
        pz_copy(i, (offset_of(NZ - 1 - i) + NZ) % NZ).start()

    def delta_of(side):
        cols = slice(side * PART, (side + 1) * PART)
        return jnp.concatenate([delta[xx, 0:1, cols] for xx in range(NX)], axis=1)


    def ready(i):
        j = NZ - 1 - i
        zz = (z + offset_of(j) + NZ) % NZ

        @pl.when(i >= 2)
        def _():
            fold_core(i - 2)

        @pl.when(i >= 4)
        def _():
            send_z(i - 4)

        vc_copy(j).wait_recv()
        keys = k_all[zz].reshape(TILE, HD)
        values = v_all[zz].reshape(TILE, HD)
        return keys, values

    def terms(keys, values, queries, cots, scored, norm, drop):
        dprob = dot(values, cots, 1, 1)
        probs = jnp.exp2(scored - norm)
        dscore = (probs * (dprob - drop)).astype(bf16)
        half = probs.astype(bf16)
        dv = dot(half, cots, 1, 0)
        dk = dot(dscore, queries, 1, 0)
        return dot(keys, dscore, 0, 0), dk, dv

    def hand_over(i, stage):
        own_rows = pl.ds(pl.multiple_of(c * HALF, HALF), HALF)
        gone_rows = pl.ds(pl.multiple_of((1 - c) * HALF, HALF), HALF)
        core_send[i] = stage[gone_rows, :].astype(bf16)
        pc_copy(i).start()
        own[i] = stage[own_rows, :]

    def grad_side(side, keys, values, store, t, stage):
        cols = pl.ds(side * SIDE, SIDE)
        dq, dk, dv = terms(
            keys, values, q_all[side].reshape(SIDE, HD), d_all[side].reshape(SIDE, HD),
            store[t, :, cols], lse[:, cols], delta_of(side),
        )
        dq_acc[:, cols] += dq
        if side == 0:
            stage[:, 0:HD] = dk * SCALE
            stage[:, HD:2 * HD] = dv
        else:
            stage[:, 0:HD] += dk * SCALE
            stage[:, HD:2 * HD] += dv

    def grad(i, store, t):
        keys, values = ready(i)
        dq, dk, dv = terms(
            keys, values, q_all[...].reshape(COLS, HD), d_all[...].reshape(COLS, HD),
            store[t], lse[...], jnp.concatenate([delta_of(0), delta_of(1)], axis=1),
        )
        dq_acc[...] += dq
        stage[:, 0:HD] = dk * SCALE
        stage[:, HD:2 * HD] = dv
        hand_over(i, stage)

    first, second = ready(0), ready(1)
    grad_side(0, *first, s_odd, NZ // 2 - 1, stage)
    grad_side(0, *second, s_even, NZ // 2 - 1, stage2)
    join(1)
    grad_side(1, *first, s_odd, NZ // 2 - 1, stage)
    hand_over(0, stage)
    grad_side(1, *second, s_even, NZ // 2 - 1, stage2)
    hand_over(1, stage2)

    def grad_pair(t, _):
        grad(2 * t, s_odd, NZ // 2 - 1 - t)

        @pl.when(t < NZ // 2 - 1)
        def _():
            grad(2 * t + 1, s_even, NZ // 2 - 1 - t)

        return 0

    lax.fori_loop(1, NZ // 2, grad_pair, 0)

    keys, values = ready(NZ - 1)

    def last(e, fresh):
        xx = (x + e) % NX
        spans = [
            pl.ds(pl.multiple_of(side * SIDE + xx * PART, PART), PART) for side in range(2)
        ]

        def both(pick, axis):
            return jnp.concatenate([pick(side) for side in range(2)], axis=axis)

        dq, dk, dv = terms(
            keys, values,
            both(lambda side: q_all[side, xx], 0), both(lambda side: d_all[side, xx], 0),
            both(lambda side: s_even[0, :, spans[side]], 1),
            both(lambda side: lse[:, spans[side]], 1), delta[xx, 0:1, :],
        )
        if fresh:
            stage[:, 0:HD] = dk * SCALE
            stage[:, HD:2 * HD] = dv
        else:
            stage[:, 0:HD] += dk * SCALE
            stage[:, HD:2 * HD] += dv
        return both(lambda side: dq_acc[:, spans[side]], 1) + dq

    for e in (2, 1, 3):
        dq_send[e - 1] = last(e, e == 2).astype(bf16)
        g_copy(e).start()
    fold_core(NZ - 2)
    send_z(NZ - 4)
    dq_sum = last(0, False)
    hand_over(NZ - 1, stage)

    fold_core(NZ - 1)
    send_z(NZ - 3)
    send_z(NZ - 2)

    for e in range(1, NX):
        g_copy(e).wait_recv()
        dq_sum = dq_sum + dq_got[e - 1].astype(f32)
    dq_rows = jnp.transpose(dq_sum * SCALE).astype(bf16)
    for h in range(HEADS):
        dq_out[:, h * HD:(h + 1) * HD] = dq_rows[h * ROWS:(h + 1) * ROWS, :]

    dq_store = pltpu.make_async_copy(dq_out, dq_hbm, ios.at[0])
    dq_store.start()
    kv_sum = fold_y(NZ - 1)
    for e in range(1, NZ):
        pz_copy(0, e).wait_recv()
        kv_sum = kv_sum + z_got[e - 1].astype(f32)
    dk_out[...] = kv_sum[:, 0:HD].astype(bf16)
    dv_out[...] = kv_sum[:, HD:2 * HD].astype(bf16)
    dk_store = pltpu.make_async_copy(dk_out, dk_hbm, ios.at[1])
    dv_store = pltpu.make_async_copy(dv_out, dv_hbm, ios.at[2])
    dk_store.start()
    dv_store.start()

    for e in range(1, NX):
        q_copy(0, e).wait_send()
        q_copy(1, e).wait_send()
        d_copy(e).wait_send()
        e_copy(e).wait_send()
        l_copy(0, e).wait_send()
        l_copy(1, e).wait_send()
        g_copy(e).wait_send()
    for e in range(1, NZ):
        kz_copy(e).wait_send()
        vz_copy(e).wait_send()
        pz_copy(0, e).wait_send()

    def drain(j, _):
        for e in range(1, NY):
            ky_copy(j, e).wait_send()
            vy_copy(j, e).wait_send()
            py_copy(j, e).wait_send()
        kc_copy(j).wait_send()
        vc_copy(j).wait_send()
        pc_copy(j).wait_send()
        return 0

    lax.fori_loop(0, NZ, drain, 0)
    dq_store.wait()
    dk_store.wait()
    dv_store.wait()


def local(queries, key_vecs, value_vecs, outputs, out_grad, positions):
    blocks = positions.reshape(-1, NC * ROWS)
    hbm = pl.BlockSpec(memory_space=pl.ANY)
    dma = pltpu.SemaphoreType.DMA
    V = pltpu.VMEM
    return pl.pallas_call(
        kernel,
        out_shape=(
            jax.ShapeDtypeStruct((ROWS, HEADS * HD), bf16),
            jax.ShapeDtypeStruct((ROWS, HD), bf16),
            jax.ShapeDtypeStruct((ROWS, HD), bf16),
        ),
        in_specs=[hbm] * 6,
        out_specs=(hbm, hbm, hbm),
        scratch_shapes=[
            V((NX * NY * NZ, NC * ROWS), jnp.int32),
            V((ROWS, HEADS * HD), bf16), V((ROWS, HEADS * HD), bf16), V((ROWS, HEADS * HD), bf16),
            V((ROWS, HEADS * HD), bf16), V((ROWS, HD), bf16), V((ROWS, HD), bf16), dma((6,)),
            V((2, NX, PART, HD), bf16), V((2, NX, PART, HD), bf16),
            V((NX, 8, WIDE), f32),
            V((2, 8, HD), f32), V((2, NX - 1, 8, HD), f32), V((1, COLS), f32),
            V((NZ, NC, NY, ROWS, HD), bf16), V((NZ, NC, NY, ROWS, HD), bf16),
            V((NZ * TILE, HD), bf16), V((COLS, HD), bf16),
            V((NZ // 2, TILE, COLS), f32), V((NZ // 2, TILE, COLS), f32),
            V((8, COLS), f32), V((8, COLS), f32),
            V((HD, COLS), f32), V((NX - 1, HD, WIDE), bf16), V((NX - 1, HD, WIDE), bf16),
            V((TILE, 2 * HD), f32), V((TILE, 2 * HD), f32),
            V((NZ, HALF, 2 * HD), f32),
            V((NZ, HALF, 2 * HD), bf16), V((NZ, HALF, 2 * HD), bf16),
            V((NZ, NY, ROWS, 2 * HD), bf16), V((NZ, NY - 1, ROWS, 2 * HD), bf16),
            V((NZ, ROWS, 2 * HD), bf16), V((NZ - 1, ROWS, 2 * HD), bf16),
        ]
        + [dma((2, NX - 1))] * 2 + [dma((NX - 1,))] * 4 + [dma((2, NX - 1))] * 2 + [dma((NX - 1,))] * 2
        + [dma((NZ - 1,)), dma((NZ - 1,)), dma((NZ, NY - 1)), dma((NZ, NY - 1)), dma((NZ,)), dma((NZ,))] * 2
        + [dma((NZ,)), dma((NZ,)), dma((NZ, NY - 1)), dma((NZ, NY - 1)), dma((NZ - 1,)), dma((NZ - 1,))],
        compiler_params=pltpu.CompilerParams(
            collective_id=0, has_side_effects=True, vmem_limit_bytes=62 * 2**20
        ),
        cost_estimate=pl.CostEstimate(
            flops=12 * COLS * NZ * TILE * HD, bytes_accessed=1 << 20, transcendentals=2 * COLS * NZ * TILE
        ),
    )(blocks, queries, key_vecs, value_vecs, outputs, out_grad)


def solution(mesh):
    rows = P(("pb", "ka"), None)
    return jax.shard_map(
        local,
        mesh=mesh,
        in_specs=(rows, rows, rows, rows, rows, P()),
        out_specs=(rows, rows, rows),
        check_vma=False,
    )
```

```python
import math

import jax
import jax.numpy as jnp
from jax import lax
from jax.experimental import pallas as pl
from jax.experimental.pallas import tpu as pltpu
from jax.sharding import PartitionSpec as P

HEADS = 8
HD = 128
NX, NY, NZ, NC = 4, 4, 8, 2
ROWS = 64
WIDE = HEADS * ROWS
COLS = NX * WIDE
PART = WIDE // 2
SIDE = COLS // 2
TILE = NC * NY * ROWS
AHEAD = 2
HALF = NY * ROWS

HIDDEN = -1e30
FLOOR = -1e20
SCALE = HD ** -0.5
LOG2E = math.log2(math.e)

f32 = jnp.float32
bf16 = jnp.bfloat16
MESH = pl.DeviceIdType.MESH


def dot(left, right, cl, cr):
    return lax.dot_general(
        left, right, (((cl,), (cr,)), ((), ())), preferred_element_type=f32
    )


def where_is(x, y, z, c):
    return {"pb": y * 4 + z // 2, "ka": (z % 2) * 8 + x * 2 + c}


def offset_of(j):
    return ((j + 1) // 2) * (2 * (j % 2) - 1)


def kernel(
    p_hbm, q_hbm, k_hbm, v_hbm, o_hbm, d_hbm,
    dq_hbm, dk_hbm, dv_hbm,
    p_in, q_in, o_in, d_in, dq_out, dk_out, dv_out, ios,
    q_all, d_all, delta, lse_own, lse_got, lse,
    k_all, v_all, k_mask, q_mask,
    s_even, s_odd, top, total,
    dq_acc, dq_send, dq_got, stage, stage2,
    own, core_send, core_got, y_send, y_got, z_send, z_got,
    qs, qr, ds, dr, es, er, ls, lr, gs, gr,
    kzs, kzr, kys, kyr, kcs, kcr,
    vzs, vzr, vys, vyr, vcs, vcr,
    pcs, pcr, pys, pyr, pzs, pzr,
):
    pb, ka = lax.axis_index("pb"), lax.axis_index("ka")
    y = pb // 4
    z = (pb % 4) * 2 + ka // 8
    x = (ka // 2) % 4
    c = ka % 2

    def send(src, dst, ssem, rsem, to):
        return pltpu.make_async_remote_copy(
            src_ref=src, dst_ref=dst, send_sem=ssem, recv_sem=rsem,
            device_id=to, device_id_type=MESH,
        )

    core_peer = where_is(x, y, z, 1 - c)

    def x_peer(e):
        return where_is((x + e) % NX, y, z, c)

    def y_peer(e):
        return where_is(x, (y + e) % NY, z, c)

    def z_peer(e):
        return where_is(x, y, (z + e) % NZ, c)

    barrier = pltpu.get_barrier_semaphore()
    peers = [core_peer]
    peers += [x_peer(e) for e in range(1, NX)]
    peers += [y_peer(e) for e in range(1, NY)]
    peers += [z_peer(e) for e in range(1, NZ)]
    for peer in peers:
        pl.semaphore_signal(barrier, inc=1, device_id=peer, device_id_type=MESH)

    loads = [
        pltpu.make_async_copy(src, dst, ios.at[n])
        for n, (src, dst) in enumerate((
            (q_hbm, q_in), (k_hbm, k_all.at[z, c, y]), (d_hbm, d_in),
            (v_hbm, v_all.at[z, c, y]), (o_hbm, o_in), (p_hbm, p_in),
        ))
    ]
    for load in loads:
        load.start()
    for load in loads:
        load.wait()
    q = q_in[...]
    d = d_in[...]
    for h in range(HEADS):
        rows = pl.ds((h % 4) * ROWS, ROWS)
        q_all[h // 4, x, rows, :] = q[:, h * HD:(h + 1) * HD]
        d_all[h // 4, x, rows, :] = d[:, h * HD:(h + 1) * HD]

    pl.semaphore_wait(barrier, len(peers))

    def q_copy(side, e):
        part = q_all.at[side, x]
        return send(part, part, qs.at[side, e - 1], qr.at[side, e - 1], x_peer(e))

    def d_copy(e):
        part = d_all.at[:, x]
        return send(part, part, ds.at[e - 1], dr.at[e - 1], x_peer(e))

    def e_copy(e):
        return send(delta.at[x], delta.at[x], es.at[e - 1], er.at[e - 1], x_peer(e))

    def l_copy(side, e):
        return send(
            lse_own.at[side], lse_got.at[side, e - 1],
            ls.at[side, e - 1], lr.at[side, e - 1], x_peer(e),
        )

    def g_copy(e):
        return send(dq_send.at[e - 1], dq_got.at[e - 1], gs.at[e - 1], gr.at[e - 1], x_peer(e))

    def kz_copy(e):
        own_k = k_all.at[z, c, y]
        return send(own_k, own_k, kzs.at[e - 1], kzr.at[e - 1], z_peer(e))

    def vz_copy(e):
        own_v = v_all.at[z, c, y]
        return send(own_v, own_v, vzs.at[e - 1], vzr.at[e - 1], z_peer(e))

    def ky_copy(j, e):
        part = k_all.at[(z + offset_of(j) + NZ) % NZ, c, y]
        return send(part, part, kys.at[j, e - 1], kyr.at[j, e - 1], y_peer(e))

    def vy_copy(j, e):
        part = v_all.at[(z + offset_of(j) + NZ) % NZ, c, y]
        return send(part, part, vys.at[j, e - 1], vyr.at[j, e - 1], y_peer(e))

    def kc_copy(j):
        part = k_all.at[(z + offset_of(j) + NZ) % NZ, c]
        return send(part, part, kcs.at[j], kcr.at[j], core_peer)

    def vc_copy(j):
        part = v_all.at[(z + offset_of(j) + NZ) % NZ, c]
        return send(part, part, vcs.at[j], vcr.at[j], core_peer)

    for e in range(1, NX):
        q_copy(0, e).start()
    for e in (1, 7, 2, 6, 3, 5, 4):
        kz_copy(e).start()
    for e in range(1, NY):
        ky_copy(0, e).start()
    for e in range(1, NX):
        q_copy(1, e).start()
    for e in range(1, NX):
        d_copy(e).start()

    row = lax.broadcasted_iota(jnp.int32, (ROWS, HD), 0)
    lane = lax.broadcasted_iota(jnp.int32, (ROWS, HD), 1)

    def start(xx, yy, zz):
        block = (yy * 4 + zz // 2) * 8 + (zz % 2) * 4 + xx
        return p_in[pl.ds(block, 1), 0:1]

    limit = jnp.full((ROWS, HD), 2 ** 30, jnp.int32)
    for xx in range(NX):
        limit = jnp.where(lane == ROWS + xx, start(xx, y, z), limit)

    def mask_keys(n, _):
        j, cc, yy = n // (NC * NY), (n // NY) % NC, n % NY
        zz = (z + offset_of(j) + NZ) % NZ
        at = pl.ds(pl.multiple_of(n * ROWS, ROWS), ROWS)
        k_mask[at, :] = jnp.where(start(x, yy, zz) > limit, HIDDEN, 0.0).astype(bf16)
        return 0

    lax.fori_loop(0, NZ * NC * NY, mask_keys, 0)
    for cc in range(NC):
        at = pl.ds(pl.multiple_of((cc * NY + y) * ROWS, ROWS), ROWS)
        later = (lane < ROWS) & (row + cc * ROWS > lane + c * ROWS)
        k_mask[at, :] = jnp.where(
            later | (start(x, y, z) > limit), HIDDEN, 0.0
        ).astype(bf16)
    for side in range(2):
        for xx in range(NX):
            mine = (lane == ROWS + xx) | ((lane == row) & (x == xx))
            one = jnp.where(mine, 1.0, 0.0).astype(bf16)
            for h in range(4):
                q_mask[pl.ds(side * SIDE + xx * PART + h * ROWS, ROWS), :] = one

    top[...] = jnp.full_like(top, FLOOR)
    total[...] = jnp.zeros_like(total)
    dq_acc[...] = jnp.zeros_like(dq_acc)

    def forward_keys(j, _):
        arrived = (NZ - offset_of(j)) % NZ
        kz_copy(arrived).wait_recv()
        for e in range(1, NY):
            ky_copy(j, e).start()
        return 0

    def share_keys(j):
        for e in range(1, NY):
            ky_copy(j, e).wait_recv()
        kc_copy(j).start()

    lax.fori_loop(1, 3, forward_keys, 0)
    share_keys(0)
    lax.fori_loop(3, 5, forward_keys, 0)
    share_keys(1)
    for e in (1, 7, 2, 6, 3, 5, 4):
        vz_copy(e).start()

    o = o_in[...].astype(f32) * d.astype(f32)
    prod = jnp.concatenate([o[:, h * HD:(h + 1) * HD] for h in range(HEADS)], axis=0)
    high = prod.astype(bf16)
    low = (prod - high.astype(f32)).astype(bf16)
    ones = jnp.ones((8, HD), bf16)
    delta[x] = dot(ones, high, 1, 1) + dot(ones, low, 1, 1)
    for e in range(1, NX):
        e_copy(e).start()

    lax.fori_loop(5, NZ, forward_keys, 0)
    for j in range(2, AHEAD):
        share_keys(j)
    for e in range(1, NX):
        q_copy(0, e).wait_recv()

    def forward_values(j):
        @pl.when(j > 0)
        def _():
            vz_copy((NZ - offset_of(j)) % NZ).wait_recv()

        for e in range(1, NY):
            vy_copy(j, e).start()

    def share_value(j):
        for e in range(1, NY):
            vy_copy(j, e).wait_recv()
        vc_copy(j).start()

    def share_values(j):
        @pl.when(j >= 2)
        def _():
            share_value(NZ + 1 - j)

        @pl.when(j >= NZ - 2)
        def _():
            share_value(NZ - 1 - j)

    def arrive(j):
        @pl.when(j < NZ - AHEAD)
        def _():
            share_keys(j + AHEAD)

        @pl.when(j >= NZ // 2)
        def _():
            forward_values(2 * NZ - 1 - 2 * j)
            forward_values(2 * NZ - 2 - 2 * j)

        kc_copy(j).wait_recv()

    def statistics(side, prepare):
        cols = pl.ds(side * SIDE, SIDE)
        queries = jnp.concatenate(
            [q_all[side].reshape(SIDE, HD), q_mask[cols, :]], axis=1
        )

        def scores(j, store, t):
            zz = (z + offset_of(j) + NZ) % NZ
            at = pl.ds(pl.multiple_of(j * TILE, TILE), TILE)
            keys = jnp.concatenate([k_all[zz].reshape(TILE, HD), k_mask[at, :]], axis=1)
            raw = dot(keys, queries, 1, 1) * (SCALE * LOG2E)
            store[t, :, cols] = raw
            return jnp.max(raw.reshape(TILE // 8, 8, SIDE), axis=0)

        def sums(store, t, high):
            part = store[t, :, cols].reshape(TILE // 8, 8, SIDE)
            return jnp.sum(jnp.exp2(part - high[None]), axis=0)

        def step(j, store, t, before, s):
            prepare(j)
            high = top[:, cols]
            seen = scores(j, store, t)
            run = total[:, cols] + sums(before, s, high)
            new = jnp.maximum(high, seen)
            total[:, cols] = run * jnp.exp2(high - new)
            top[:, cols] = new

        prepare(jnp.int32(0))
        top[:, cols] = jnp.maximum(top[:, cols], scores(0, s_even, 0))

        def pair(t, _):
            step(2 * t + 1, s_odd, t, s_even, t)

            @pl.when(t < NZ // 2 - 1)
            def _():
                step(2 * t + 2, s_even, t + 1, s_odd, t)

            return 0

        lax.fori_loop(0, NZ // 2, pair, 0)
        high = top[:, cols]
        run = total[:, cols] + sums(s_odd, NZ // 2 - 1, high)
        peak = jnp.max(high, axis=0, keepdims=True)
        mass = jnp.sum(run * jnp.exp2(high - peak), axis=0, keepdims=True)
        mine = jnp.where(mass > 0.0, peak + jnp.log2(mass), FLOOR)
        for n in range(8):
            lse_own[side, n:n + 1, :] = mine[:, n * HD:(n + 1) * HD]
        for e in range(1, NX):
            l_copy(side, e).start()

    def join(side):
        for e in range(1, NX):
            l_copy(side, e).wait_recv()
        parts = [lse_own[side]] + [lse_got[side, e] for e in range(NX - 1)]
        peak = jnp.maximum(jnp.maximum(parts[0], parts[1]), jnp.maximum(parts[2], parts[3]))
        joint = peak + jnp.log2(sum(jnp.exp2(part - peak) for part in parts))
        for n in range(8):
            lse[:, side * SIDE + n * HD:side * SIDE + (n + 1) * HD] = joint[n:n + 1, :]

    statistics(0, arrive)
    for e in range(1, NX):
        q_copy(1, e).wait_recv()
    statistics(1, share_values)

    for e in range(1, NX):
        d_copy(e).wait_recv()
        e_copy(e).wait_recv()
    join(0)

    def pc_copy(i):
        return send(core_send.at[i], core_got.at[i], pcs.at[i], pcr.at[i], core_peer)

    def py_copy(i, e):
        return send(
            y_send.at[i, (y + e) % NY], y_got.at[i, e - 1],
            pys.at[i, e - 1], pyr.at[i, e - 1], y_peer(e),
        )

    def pz_copy(i, e):
        return send(z_send.at[i], z_got.at[e - 1], pzs.at[e - 1], pzr.at[e - 1], z_peer(e))

    def fold_core(i):
        pc_copy(i).wait_recv()
        both = own[i] + core_got[i].astype(f32)
        y_send[i] = both.astype(bf16).reshape(NY, ROWS, 2 * HD)
        for e in range(1, NY):
            py_copy(i, e).start()

    def fold_y(i):
        for e in range(1, NY):
            py_copy(i, e).wait_recv()
        part = y_send[i, y].astype(f32)
        for e in range(NY - 1):
            part = part + y_got[i, e].astype(f32)
        return part

    def send_z(i):
        z_send[i] = fold_y(i).astype(bf16)
        pz_copy(i, (offset_of(NZ - 1 - i) + NZ) % NZ).start()

    def delta_of(side):
        cols = slice(side * PART, (side + 1) * PART)
        return jnp.concatenate([delta[xx, 0:1, cols] for xx in range(NX)], axis=1)


    def ready(i):
        j = NZ - 1 - i
        zz = (z + offset_of(j) + NZ) % NZ

        @pl.when(i >= 2)
        def _():
            fold_core(i - 2)

        @pl.when(i >= 4)
        def _():
            send_z(i - 4)

        vc_copy(j).wait_recv()
        keys = k_all[zz].reshape(TILE, HD)
        values = v_all[zz].reshape(TILE, HD)
        return keys, values

    def terms(keys, values, queries, cots, scored, norm, drop):
        dprob = dot(values, cots, 1, 1)
        probs = jnp.exp2(scored - norm)
        dscore = (probs * (dprob - drop)).astype(bf16)
        half = probs.astype(bf16)
        dv = dot(half, cots, 1, 0)
        dk = dot(dscore, queries, 1, 0)
        return dot(keys, dscore, 0, 0), dk, dv

    def hand_over(i, stage):
        own_rows = pl.ds(pl.multiple_of(c * HALF, HALF), HALF)
        gone_rows = pl.ds(pl.multiple_of((1 - c) * HALF, HALF), HALF)
        core_send[i] = stage[gone_rows, :].astype(bf16)
        pc_copy(i).start()
        own[i] = stage[own_rows, :]

    def grad_side(side, keys, values, store, t, stage):
        cols = pl.ds(side * SIDE, SIDE)
        dq, dk, dv = terms(
            keys, values, q_all[side].reshape(SIDE, HD), d_all[side].reshape(SIDE, HD),
            store[t, :, cols], lse[:, cols], delta_of(side),
        )
        dq_acc[:, cols] += dq
        if side == 0:
            stage[:, 0:HD] = dk * SCALE
            stage[:, HD:2 * HD] = dv
        else:
            stage[:, 0:HD] += dk * SCALE
            stage[:, HD:2 * HD] += dv

    def grad(i, store, t):
        keys, values = ready(i)
        dq, dk, dv = terms(
            keys, values, q_all[...].reshape(COLS, HD), d_all[...].reshape(COLS, HD),
            store[t], lse[...], jnp.concatenate([delta_of(0), delta_of(1)], axis=1),
        )
        dq_acc[...] += dq
        stage[:, 0:HD] = dk * SCALE
        stage[:, HD:2 * HD] = dv
        hand_over(i, stage)

    first, second = ready(0), ready(1)
    grad_side(0, *first, s_odd, NZ // 2 - 1, stage)
    grad_side(0, *second, s_even, NZ // 2 - 1, stage2)
    join(1)
    grad_side(1, *first, s_odd, NZ // 2 - 1, stage)
    hand_over(0, stage)
    grad_side(1, *second, s_even, NZ // 2 - 1, stage2)
    hand_over(1, stage2)

    def grad_pair(t, _):
        grad(2 * t, s_odd, NZ // 2 - 1 - t)

        @pl.when(t < NZ // 2 - 1)
        def _():
            grad(2 * t + 1, s_even, NZ // 2 - 1 - t)

        return 0

    lax.fori_loop(1, NZ // 2, grad_pair, 0)

    keys, values = ready(NZ - 1)

    def last(e, fresh):
        xx = (x + e) % NX
        spans = [
            pl.ds(pl.multiple_of(side * SIDE + xx * PART, PART), PART) for side in range(2)
        ]

        def both(pick, axis):
            return jnp.concatenate([pick(side) for side in range(2)], axis=axis)

        dq, dk, dv = terms(
            keys, values,
            both(lambda side: q_all[side, xx], 0), both(lambda side: d_all[side, xx], 0),
            both(lambda side: s_even[0, :, spans[side]], 1),
            both(lambda side: lse[:, spans[side]], 1), delta[xx, 0:1, :],
        )
        if fresh:
            stage[:, 0:HD] = dk * SCALE
            stage[:, HD:2 * HD] = dv
        else:
            stage[:, 0:HD] += dk * SCALE
            stage[:, HD:2 * HD] += dv
        return both(lambda side: dq_acc[:, spans[side]], 1) + dq

    for e in (2, 1, 3):
        dq_send[e - 1] = last(e, e == 2).astype(bf16)
        g_copy(e).start()
    fold_core(NZ - 2)
    send_z(NZ - 4)
    dq_sum = last(0, False)
    hand_over(NZ - 1, stage)

    fold_core(NZ - 1)
    send_z(NZ - 3)
    send_z(NZ - 2)

    for e in range(1, NX):
        g_copy(e).wait_recv()
        dq_sum = dq_sum + dq_got[e - 1].astype(f32)
    dq_rows = jnp.transpose(dq_sum * SCALE).astype(bf16)
    for h in range(HEADS):
        dq_out[:, h * HD:(h + 1) * HD] = dq_rows[h * ROWS:(h + 1) * ROWS, :]

    dq_store = pltpu.make_async_copy(dq_out, dq_hbm, ios.at[0])
    dq_store.start()
    kv_sum = fold_y(NZ - 1)
    for e in range(1, NZ):
        pz_copy(0, e).wait_recv()
        kv_sum = kv_sum + z_got[e - 1].astype(f32)
    dk_out[...] = kv_sum[:, 0:HD].astype(bf16)
    dv_out[...] = kv_sum[:, HD:2 * HD].astype(bf16)
    dk_store = pltpu.make_async_copy(dk_out, dk_hbm, ios.at[1])
    dv_store = pltpu.make_async_copy(dv_out, dv_hbm, ios.at[2])
    dk_store.start()
    dv_store.start()

    for e in range(1, NX):
        q_copy(0, e).wait_send()
        q_copy(1, e).wait_send()
        d_copy(e).wait_send()
        e_copy(e).wait_send()
        l_copy(0, e).wait_send()
        l_copy(1, e).wait_send()
        g_copy(e).wait_send()
    for e in range(1, NZ):
        kz_copy(e).wait_send()
        vz_copy(e).wait_send()
        pz_copy(0, e).wait_send()

    def drain(j, _):
        for e in range(1, NY):
            ky_copy(j, e).wait_send()
            vy_copy(j, e).wait_send()
            py_copy(j, e).wait_send()
        kc_copy(j).wait_send()
        vc_copy(j).wait_send()
        pc_copy(j).wait_send()
        return 0

    lax.fori_loop(0, NZ, drain, 0)
    dq_store.wait()
    dk_store.wait()
    dv_store.wait()


def local(queries, key_vecs, value_vecs, outputs, out_grad, positions):
    blocks = positions.reshape(-1, NC * ROWS)
    hbm = pl.BlockSpec(memory_space=pl.ANY)
    dma = pltpu.SemaphoreType.DMA
    V = pltpu.VMEM
    return pl.pallas_call(
        kernel,
        out_shape=(
            jax.ShapeDtypeStruct((ROWS, HEADS * HD), bf16),
            jax.ShapeDtypeStruct((ROWS, HD), bf16),
            jax.ShapeDtypeStruct((ROWS, HD), bf16),
        ),
        in_specs=[hbm] * 6,
        out_specs=(hbm, hbm, hbm),
        scratch_shapes=[
            V((NX * NY * NZ, NC * ROWS), jnp.int32),
            V((ROWS, HEADS * HD), bf16), V((ROWS, HEADS * HD), bf16), V((ROWS, HEADS * HD), bf16),
            V((ROWS, HEADS * HD), bf16), V((ROWS, HD), bf16), V((ROWS, HD), bf16), dma((6,)),
            V((2, NX, PART, HD), bf16), V((2, NX, PART, HD), bf16),
            V((NX, 8, WIDE), f32),
            V((2, 8, HD), f32), V((2, NX - 1, 8, HD), f32), V((1, COLS), f32),
            V((NZ, NC, NY, ROWS, HD), bf16), V((NZ, NC, NY, ROWS, HD), bf16),
            V((NZ * TILE, HD), bf16), V((COLS, HD), bf16),
            V((NZ // 2, TILE, COLS), f32), V((NZ // 2, TILE, COLS), f32),
            V((8, COLS), f32), V((8, COLS), f32),
            V((HD, COLS), f32), V((NX - 1, HD, WIDE), bf16), V((NX - 1, HD, WIDE), bf16),
            V((TILE, 2 * HD), f32), V((TILE, 2 * HD), f32),
            V((NZ, HALF, 2 * HD), f32),
            V((NZ, HALF, 2 * HD), bf16), V((NZ, HALF, 2 * HD), bf16),
            V((NZ, NY, ROWS, 2 * HD), bf16), V((NZ, NY - 1, ROWS, 2 * HD), bf16),
            V((NZ, ROWS, 2 * HD), bf16), V((NZ - 1, ROWS, 2 * HD), bf16),
        ]
        + [dma((2, NX - 1))] * 2 + [dma((NX - 1,))] * 4 + [dma((2, NX - 1))] * 2 + [dma((NX - 1,))] * 2
        + [dma((NZ - 1,)), dma((NZ - 1,)), dma((NZ, NY - 1)), dma((NZ, NY - 1)), dma((NZ,)), dma((NZ,))] * 2
        + [dma((NZ,)), dma((NZ,)), dma((NZ, NY - 1)), dma((NZ, NY - 1)), dma((NZ - 1,)), dma((NZ - 1,))],
        compiler_params=pltpu.CompilerParams(
            collective_id=0, has_side_effects=True, vmem_limit_bytes=62 * 2**20
        ),
        cost_estimate=pl.CostEstimate(
            flops=12 * COLS * NZ * TILE * HD, bytes_accessed=1 << 20, transcendentals=2 * COLS * NZ * TILE
        ),
    )(blocks, queries, key_vecs, value_vecs, outputs, out_grad)


def solution(mesh):
    rows = P(("pb", "ka"), None)
    return jax.shard_map(
        local,
        mesh=mesh,
        in_specs=(rows, rows, rows, rows, rows, P()),
        out_specs=(rows, rows, rows),
        check_vma=False,
    )
```

```python
import math

import jax
import jax.numpy as jnp
from jax import lax
from jax.experimental import pallas as pl
from jax.experimental.pallas import tpu as pltpu
from jax.sharding import PartitionSpec as P

HEADS = 8
HD = 128
NX, NY, NZ, NC = 4, 4, 8, 2
ROWS = 64
WIDE = HEADS * ROWS
COLS = NX * WIDE
PART = WIDE // 2
SIDE = COLS // 2
TILE = NC * NY * ROWS
AHEAD = 2
HALF = NY * ROWS

HIDDEN = -1e30
FLOOR = -1e20
SCALE = HD ** -0.5
LOG2E = math.log2(math.e)

f32 = jnp.float32
bf16 = jnp.bfloat16
MESH = pl.DeviceIdType.MESH


def dot(left, right, cl, cr):
    return lax.dot_general(
        left, right, (((cl,), (cr,)), ((), ())), preferred_element_type=f32
    )


def where_is(x, y, z, c):
    return {"pb": y * 4 + z // 2, "ka": (z % 2) * 8 + x * 2 + c}


def offset_of(j):
    return ((j + 1) // 2) * (2 * (j % 2) - 1)


def kernel(
    p_hbm, q_hbm, k_hbm, v_hbm, o_hbm, d_hbm,
    dq_hbm, dk_hbm, dv_hbm,
    p_in, q_in, o_in, d_in, dq_out, dk_out, dv_out, ios,
    q_all, d_all, delta, lse_own, lse_got, lse,
    k_all, v_all, k_mask, q_mask,
    s_even, s_odd, top, total,
    dq_acc, dq_send, dq_got, stage, stage2,
    own, core_send, core_got, y_send, y_got, z_send, z_got,
    qs, qr, ds, dr, es, er, ls, lr, gs, gr,
    kzs, kzr, kys, kyr, kcs, kcr,
    vzs, vzr, vys, vyr, vcs, vcr,
    pcs, pcr, pys, pyr, pzs, pzr,
):
    pb, ka = lax.axis_index("pb"), lax.axis_index("ka")
    y = pb // 4
    z = (pb % 4) * 2 + ka // 8
    x = (ka // 2) % 4
    c = ka % 2

    def send(src, dst, ssem, rsem, to):
        return pltpu.make_async_remote_copy(
            src_ref=src, dst_ref=dst, send_sem=ssem, recv_sem=rsem,
            device_id=to, device_id_type=MESH,
        )

    core_peer = where_is(x, y, z, 1 - c)

    def x_peer(e):
        return where_is((x + e) % NX, y, z, c)

    def y_peer(e):
        return where_is(x, (y + e) % NY, z, c)

    def z_peer(e):
        return where_is(x, y, (z + e) % NZ, c)

    barrier = pltpu.get_barrier_semaphore()
    peers = [core_peer]
    peers += [x_peer(e) for e in range(1, NX)]
    peers += [y_peer(e) for e in range(1, NY)]
    peers += [z_peer(e) for e in range(1, NZ)]
    for peer in peers:
        pl.semaphore_signal(barrier, inc=1, device_id=peer, device_id_type=MESH)

    loads = [
        pltpu.make_async_copy(src, dst, ios.at[n])
        for n, (src, dst) in enumerate((
            (q_hbm, q_in), (k_hbm, k_all.at[z, c, y]), (d_hbm, d_in),
            (v_hbm, v_all.at[z, c, y]), (o_hbm, o_in), (p_hbm, p_in),
        ))
    ]
    for load in loads:
        load.start()
    for load in loads[:2]:
        load.wait()
    q = q_in[...]
    for h in range(HEADS):
        rows = pl.ds((h % 4) * ROWS, ROWS)
        q_all[h // 4, x, rows, :] = q[:, h * HD:(h + 1) * HD]

    pl.semaphore_wait(barrier, len(peers))

    def q_copy(side, e):
        part = q_all.at[side, x]
        return send(part, part, qs.at[side, e - 1], qr.at[side, e - 1], x_peer(e))

    def d_copy(e):
        part = d_all.at[:, x]
        return send(part, part, ds.at[e - 1], dr.at[e - 1], x_peer(e))

    def e_copy(e):
        return send(delta.at[x], delta.at[x], es.at[e - 1], er.at[e - 1], x_peer(e))

    def l_copy(side, e):
        return send(
            lse_own.at[side], lse_got.at[side, e - 1],
            ls.at[side, e - 1], lr.at[side, e - 1], x_peer(e),
        )

    def g_copy(e):
        return send(dq_send.at[e - 1], dq_got.at[e - 1], gs.at[e - 1], gr.at[e - 1], x_peer(e))

    def kz_copy(e):
        own_k = k_all.at[z, c, y]
        return send(own_k, own_k, kzs.at[e - 1], kzr.at[e - 1], z_peer(e))

    def vz_copy(e):
        own_v = v_all.at[z, c, y]
        return send(own_v, own_v, vzs.at[e - 1], vzr.at[e - 1], z_peer(e))

    def ky_copy(j, e):
        part = k_all.at[(z + offset_of(j) + NZ) % NZ, c, y]
        return send(part, part, kys.at[j, e - 1], kyr.at[j, e - 1], y_peer(e))

    def vy_copy(j, e):
        part = v_all.at[(z + offset_of(j) + NZ) % NZ, c, y]
        return send(part, part, vys.at[j, e - 1], vyr.at[j, e - 1], y_peer(e))

    def kc_copy(j):
        part = k_all.at[(z + offset_of(j) + NZ) % NZ, c]
        return send(part, part, kcs.at[j], kcr.at[j], core_peer)

    def vc_copy(j):
        part = v_all.at[(z + offset_of(j) + NZ) % NZ, c]
        return send(part, part, vcs.at[j], vcr.at[j], core_peer)

    for e in range(1, NX):
        q_copy(0, e).start()
    for e in (1, 7, 2, 6, 3, 5, 4):
        kz_copy(e).start()
    for e in range(1, NY):
        ky_copy(0, e).start()
    for e in range(1, NX):
        q_copy(1, e).start()
    for load in loads[2:]:
        load.wait()
    d = d_in[...]
    for h in range(HEADS):
        rows = pl.ds((h % 4) * ROWS, ROWS)
        d_all[h // 4, x, rows, :] = d[:, h * HD:(h + 1) * HD]
    for e in range(1, NX):
        d_copy(e).start()

    row = lax.broadcasted_iota(jnp.int32, (ROWS, HD), 0)
    lane = lax.broadcasted_iota(jnp.int32, (ROWS, HD), 1)

    def start(xx, yy, zz):
        block = (yy * 4 + zz // 2) * 8 + (zz % 2) * 4 + xx
        return p_in[pl.ds(block, 1), 0:1]

    limit = jnp.full((ROWS, HD), 2 ** 30, jnp.int32)
    for xx in range(NX):
        limit = jnp.where(lane == ROWS + xx, start(xx, y, z), limit)

    def mask_keys(n, _):
        j, cc, yy = n // (NC * NY), (n // NY) % NC, n % NY
        zz = (z + offset_of(j) + NZ) % NZ
        at = pl.ds(pl.multiple_of(n * ROWS, ROWS), ROWS)
        k_mask[at, :] = jnp.where(start(x, yy, zz) > limit, HIDDEN, 0.0).astype(bf16)
        return 0

    lax.fori_loop(0, NZ * NC * NY, mask_keys, 0)
    for cc in range(NC):
        at = pl.ds(pl.multiple_of((cc * NY + y) * ROWS, ROWS), ROWS)
        later = (lane < ROWS) & (row + cc * ROWS > lane + c * ROWS)
        k_mask[at, :] = jnp.where(
            later | (start(x, y, z) > limit), HIDDEN, 0.0
        ).astype(bf16)
    for side in range(2):
        for xx in range(NX):
            mine = (lane == ROWS + xx) | ((lane == row) & (x == xx))
            one = jnp.where(mine, 1.0, 0.0).astype(bf16)
            for h in range(4):
                q_mask[pl.ds(side * SIDE + xx * PART + h * ROWS, ROWS), :] = one

    top[...] = jnp.full_like(top, FLOOR)
    total[...] = jnp.zeros_like(total)
    dq_acc[...] = jnp.zeros_like(dq_acc)

    def forward_keys(j, _):
        arrived = (NZ - offset_of(j)) % NZ
        kz_copy(arrived).wait_recv()
        for e in range(1, NY):
            ky_copy(j, e).start()
        return 0

    def share_keys(j):
        for e in range(1, NY):
            ky_copy(j, e).wait_recv()
        kc_copy(j).start()

    lax.fori_loop(1, 3, forward_keys, 0)
    share_keys(0)
    lax.fori_loop(3, 5, forward_keys, 0)
    share_keys(1)
    for e in (1, 7, 2, 6, 3, 5, 4):
        vz_copy(e).start()

    o = o_in[...].astype(f32) * d.astype(f32)
    prod = jnp.concatenate([o[:, h * HD:(h + 1) * HD] for h in range(HEADS)], axis=0)
    high = prod.astype(bf16)
    low = (prod - high.astype(f32)).astype(bf16)
    ones = jnp.ones((8, HD), bf16)
    delta[x] = dot(ones, high, 1, 1) + dot(ones, low, 1, 1)
    for e in range(1, NX):
        e_copy(e).start()

    lax.fori_loop(5, NZ, forward_keys, 0)
    for j in range(2, AHEAD):
        share_keys(j)
    for e in range(1, NX):
        q_copy(0, e).wait_recv()

    def forward_values(j):
        @pl.when(j > 0)
        def _():
            vz_copy((NZ - offset_of(j)) % NZ).wait_recv()

        for e in range(1, NY):
            vy_copy(j, e).start()

    def share_value(j):
        for e in range(1, NY):
            vy_copy(j, e).wait_recv()
        vc_copy(j).start()

    def share_values(j):
        @pl.when(j >= 2)
        def _():
            share_value(NZ + 1 - j)

        @pl.when(j >= NZ - 2)
        def _():
            share_value(NZ - 1 - j)

    def arrive(j):
        @pl.when(j < NZ - AHEAD)
        def _():
            share_keys(j + AHEAD)

        @pl.when(j >= NZ // 2)
        def _():
            forward_values(2 * NZ - 1 - 2 * j)
            forward_values(2 * NZ - 2 - 2 * j)

        kc_copy(j).wait_recv()

    def statistics(side, prepare):
        cols = pl.ds(side * SIDE, SIDE)
        queries = jnp.concatenate(
            [q_all[side].reshape(SIDE, HD), q_mask[cols, :]], axis=1
        )

        def scores(j, store, t):
            zz = (z + offset_of(j) + NZ) % NZ
            at = pl.ds(pl.multiple_of(j * TILE, TILE), TILE)
            keys = jnp.concatenate([k_all[zz].reshape(TILE, HD), k_mask[at, :]], axis=1)
            raw = dot(keys, queries, 1, 1) * (SCALE * LOG2E)
            store[t, :, cols] = raw
            return jnp.max(raw.reshape(TILE // 8, 8, SIDE), axis=0)

        def sums(store, t, high):
            part = store[t, :, cols].reshape(TILE // 8, 8, SIDE)
            return jnp.sum(jnp.exp2(part - high[None]), axis=0)

        def step(j, store, t, before, s):
            prepare(j)
            high = top[:, cols]
            seen = scores(j, store, t)
            run = total[:, cols] + sums(before, s, high)
            new = jnp.maximum(high, seen)
            total[:, cols] = run * jnp.exp2(high - new)
            top[:, cols] = new

        prepare(jnp.int32(0))
        top[:, cols] = jnp.maximum(top[:, cols], scores(0, s_even, 0))

        def pair(t, _):
            step(2 * t + 1, s_odd, t, s_even, t)

            @pl.when(t < NZ // 2 - 1)
            def _():
                step(2 * t + 2, s_even, t + 1, s_odd, t)

            return 0

        lax.fori_loop(0, NZ // 2, pair, 0)
        high = top[:, cols]
        run = total[:, cols] + sums(s_odd, NZ // 2 - 1, high)
        peak = jnp.max(high, axis=0, keepdims=True)
        mass = jnp.sum(run * jnp.exp2(high - peak), axis=0, keepdims=True)
        mine = jnp.where(mass > 0.0, peak + jnp.log2(mass), FLOOR)
        for n in range(8):
            lse_own[side, n:n + 1, :] = mine[:, n * HD:(n + 1) * HD]
        for e in range(1, NX):
            l_copy(side, e).start()

    def join(side):
        for e in range(1, NX):
            l_copy(side, e).wait_recv()
        parts = [lse_own[side]] + [lse_got[side, e] for e in range(NX - 1)]
        peak = jnp.maximum(jnp.maximum(parts[0], parts[1]), jnp.maximum(parts[2], parts[3]))
        joint = peak + jnp.log2(sum(jnp.exp2(part - peak) for part in parts))
        for n in range(8):
            lse[:, side * SIDE + n * HD:side * SIDE + (n + 1) * HD] = joint[n:n + 1, :]

    statistics(0, arrive)
    for e in range(1, NX):
        q_copy(1, e).wait_recv()
    statistics(1, share_values)

    for e in range(1, NX):
        d_copy(e).wait_recv()
        e_copy(e).wait_recv()
    join(0)

    def pc_copy(i):
        return send(core_send.at[i], core_got.at[i], pcs.at[i], pcr.at[i], core_peer)

    def py_copy(i, e):
        return send(
            y_send.at[i, (y + e) % NY], y_got.at[i, e - 1],
            pys.at[i, e - 1], pyr.at[i, e - 1], y_peer(e),
        )

    def pz_copy(i, e):
        return send(z_send.at[i], z_got.at[e - 1], pzs.at[e - 1], pzr.at[e - 1], z_peer(e))

    def fold_core(i):
        pc_copy(i).wait_recv()
        both = own[i] + core_got[i].astype(f32)
        y_send[i] = both.astype(bf16).reshape(NY, ROWS, 2 * HD)
        for e in range(1, NY):
            py_copy(i, e).start()

    def fold_y(i):
        for e in range(1, NY):
            py_copy(i, e).wait_recv()
        part = y_send[i, y].astype(f32)
        for e in range(NY - 1):
            part = part + y_got[i, e].astype(f32)
        return part

    def send_z(i):
        z_send[i] = fold_y(i).astype(bf16)
        pz_copy(i, (offset_of(NZ - 1 - i) + NZ) % NZ).start()

    def delta_of(side):
        cols = slice(side * PART, (side + 1) * PART)
        return jnp.concatenate([delta[xx, 0:1, cols] for xx in range(NX)], axis=1)


    def ready(i):
        j = NZ - 1 - i
        zz = (z + offset_of(j) + NZ) % NZ

        @pl.when(i >= 2)
        def _():
            fold_core(i - 2)

        @pl.when(i >= 4)
        def _():
            send_z(i - 4)

        vc_copy(j).wait_recv()
        keys = k_all[zz].reshape(TILE, HD)
        values = v_all[zz].reshape(TILE, HD)
        return keys, values

    def halves(values, cots, scored, norm, drop):
        dprob = dot(values, cots, 1, 1)
        probs = jnp.exp2(scored - norm)
        dscore = (probs * (dprob - drop)).astype(bf16)
        return dscore, probs.astype(bf16)

    def terms(keys, values, queries, cots, scored, norm, drop):
        dscore, half = halves(values, cots, scored, norm, drop)
        dv = dot(half, cots, 1, 0)
        dk = dot(dscore, queries, 1, 0)
        return dot(keys, dscore, 0, 0), dk, dv

    def hand_over(i, stage):
        own_rows = pl.ds(pl.multiple_of(c * HALF, HALF), HALF)
        gone_rows = pl.ds(pl.multiple_of((1 - c) * HALF, HALF), HALF)
        core_send[i] = stage[gone_rows, :].astype(bf16)
        pc_copy(i).start()
        own[i] = stage[own_rows, :]

    def grad_side(side, keys, values, store, t, stage):
        cols = pl.ds(side * SIDE, SIDE)
        dq, dk, dv = terms(
            keys, values, q_all[side].reshape(SIDE, HD), d_all[side].reshape(SIDE, HD),
            store[t, :, cols], lse[:, cols], delta_of(side),
        )
        dq_acc[:, cols] += dq
        if side == 0:
            stage[:, 0:HD] = dk * SCALE
            stage[:, HD:2 * HD] = dv
        else:
            stage[:, 0:HD] += dk * SCALE
            stage[:, HD:2 * HD] += dv

    def grad(i, store, t):
        keys, values = ready(i)
        dq, dk, dv = terms(
            keys, values, q_all[...].reshape(COLS, HD), d_all[...].reshape(COLS, HD),
            store[t], lse[...], jnp.concatenate([delta_of(0), delta_of(1)], axis=1),
        )
        dq_acc[...] += dq
        stage[:, 0:HD] = dk * SCALE
        stage[:, HD:2 * HD] = dv
        hand_over(i, stage)

    first, second = ready(0), ready(1)
    grad_side(0, *first, s_odd, NZ // 2 - 1, stage)
    grad_side(0, *second, s_even, NZ // 2 - 1, stage2)
    join(1)
    grad_side(1, *first, s_odd, NZ // 2 - 1, stage)
    hand_over(0, stage)
    grad_side(1, *second, s_even, NZ // 2 - 1, stage2)
    hand_over(1, stage2)

    def grad_pair(t, _):
        grad(2 * t, s_odd, NZ // 2 - 1 - t)

        @pl.when(t < NZ // 2 - 1)
        def _():
            grad(2 * t + 1, s_even, NZ // 2 - 1 - t)

        return 0

    lax.fori_loop(1, NZ // 2, grad_pair, 0)

    keys, values = ready(NZ - 1)

    def last(e, fresh):
        xx = (x + e) % NX
        spans = [
            pl.ds(pl.multiple_of(side * SIDE + xx * PART, PART), PART) for side in range(2)
        ]

        def both(pick, axis):
            return jnp.concatenate([pick(side) for side in range(2)], axis=axis)

        queries = both(lambda side: q_all[side, xx], 0)
        cots = both(lambda side: d_all[side, xx], 0)
        dscore, half = halves(
            values, cots, both(lambda side: s_even[0, :, spans[side]], 1),
            both(lambda side: lse[:, spans[side]], 1), delta[xx, 0:1, :],
        )
        dq = both(lambda side: dq_acc[:, spans[side]], 1) + dot(keys, dscore, 0, 0)
        if e > 0:
            dq_send[e - 1] = dq.astype(bf16)
            g_copy(e).start()
        dv = dot(half, cots, 1, 0)
        dk = dot(dscore, queries, 1, 0)
        if fresh:
            stage[:, 0:HD] = dk * SCALE
            stage[:, HD:2 * HD] = dv
        else:
            stage[:, 0:HD] += dk * SCALE
            stage[:, HD:2 * HD] += dv
        return dq

    for e in (2, 1, 3):
        last(e, e == 2)
    fold_core(NZ - 2)
    send_z(NZ - 4)
    dq_sum = last(0, False)
    hand_over(NZ - 1, stage)

    fold_core(NZ - 1)
    send_z(NZ - 3)
    send_z(NZ - 2)

    for e in range(1, NX):
        g_copy(e).wait_recv()
        dq_sum = dq_sum + dq_got[e - 1].astype(f32)
    dq_rows = jnp.transpose(dq_sum * SCALE).astype(bf16)
    for h in range(HEADS):
        dq_out[:, h * HD:(h + 1) * HD] = dq_rows[h * ROWS:(h + 1) * ROWS, :]

    dq_store = pltpu.make_async_copy(dq_out, dq_hbm, ios.at[0])
    dq_store.start()
    kv_sum = fold_y(NZ - 1)
    for e in range(1, NZ):
        pz_copy(0, e).wait_recv()
        kv_sum = kv_sum + z_got[e - 1].astype(f32)
    dk_out[...] = kv_sum[:, 0:HD].astype(bf16)
    dv_out[...] = kv_sum[:, HD:2 * HD].astype(bf16)
    dk_store = pltpu.make_async_copy(dk_out, dk_hbm, ios.at[1])
    dv_store = pltpu.make_async_copy(dv_out, dv_hbm, ios.at[2])
    dk_store.start()
    dv_store.start()

    for e in range(1, NX):
        q_copy(0, e).wait_send()
        q_copy(1, e).wait_send()
        d_copy(e).wait_send()
        e_copy(e).wait_send()
        l_copy(0, e).wait_send()
        l_copy(1, e).wait_send()
        g_copy(e).wait_send()
    for e in range(1, NZ):
        kz_copy(e).wait_send()
        vz_copy(e).wait_send()
        pz_copy(0, e).wait_send()

    def drain(j, _):
        for e in range(1, NY):
            ky_copy(j, e).wait_send()
            vy_copy(j, e).wait_send()
            py_copy(j, e).wait_send()
        kc_copy(j).wait_send()
        vc_copy(j).wait_send()
        pc_copy(j).wait_send()
        return 0

    lax.fori_loop(0, NZ, drain, 0)
    dq_store.wait()
    dk_store.wait()
    dv_store.wait()


def local(queries, key_vecs, value_vecs, outputs, out_grad, positions):
    blocks = positions.reshape(-1, NC * ROWS)
    hbm = pl.BlockSpec(memory_space=pl.ANY)
    dma = pltpu.SemaphoreType.DMA
    V = pltpu.VMEM
    return pl.pallas_call(
        kernel,
        out_shape=(
            jax.ShapeDtypeStruct((ROWS, HEADS * HD), bf16),
            jax.ShapeDtypeStruct((ROWS, HD), bf16),
            jax.ShapeDtypeStruct((ROWS, HD), bf16),
        ),
        in_specs=[hbm] * 6,
        out_specs=(hbm, hbm, hbm),
        scratch_shapes=[
            V((NX * NY * NZ, NC * ROWS), jnp.int32),
            V((ROWS, HEADS * HD), bf16), V((ROWS, HEADS * HD), bf16), V((ROWS, HEADS * HD), bf16),
            V((ROWS, HEADS * HD), bf16), V((ROWS, HD), bf16), V((ROWS, HD), bf16), dma((6,)),
            V((2, NX, PART, HD), bf16), V((2, NX, PART, HD), bf16),
            V((NX, 8, WIDE), f32),
            V((2, 8, HD), f32), V((2, NX - 1, 8, HD), f32), V((1, COLS), f32),
            V((NZ, NC, NY, ROWS, HD), bf16), V((NZ, NC, NY, ROWS, HD), bf16),
            V((NZ * TILE, HD), bf16), V((COLS, HD), bf16),
            V((NZ // 2, TILE, COLS), f32), V((NZ // 2, TILE, COLS), f32),
            V((8, COLS), f32), V((8, COLS), f32),
            V((HD, COLS), f32), V((NX - 1, HD, WIDE), bf16), V((NX - 1, HD, WIDE), bf16),
            V((TILE, 2 * HD), f32), V((TILE, 2 * HD), f32),
            V((NZ, HALF, 2 * HD), f32),
            V((NZ, HALF, 2 * HD), bf16), V((NZ, HALF, 2 * HD), bf16),
            V((NZ, NY, ROWS, 2 * HD), bf16), V((NZ, NY - 1, ROWS, 2 * HD), bf16),
            V((NZ, ROWS, 2 * HD), bf16), V((NZ - 1, ROWS, 2 * HD), bf16),
        ]
        + [dma((2, NX - 1))] * 2 + [dma((NX - 1,))] * 4 + [dma((2, NX - 1))] * 2 + [dma((NX - 1,))] * 2
        + [dma((NZ - 1,)), dma((NZ - 1,)), dma((NZ, NY - 1)), dma((NZ, NY - 1)), dma((NZ,)), dma((NZ,))] * 2
        + [dma((NZ,)), dma((NZ,)), dma((NZ, NY - 1)), dma((NZ, NY - 1)), dma((NZ - 1,)), dma((NZ - 1,))],
        compiler_params=pltpu.CompilerParams(
            collective_id=0, has_side_effects=True, vmem_limit_bytes=62 * 2**20
        ),
        cost_estimate=pl.CostEstimate(
            flops=12 * COLS * NZ * TILE * HD, bytes_accessed=1 << 20, transcendentals=2 * COLS * NZ * TILE
        ),
    )(blocks, queries, key_vecs, value_vecs, outputs, out_grad)


def solution(mesh):
    rows = P(("pb", "ka"), None)
    return jax.shard_map(
        local,
        mesh=mesh,
        in_specs=(rows, rows, rows, rows, rows, P()),
        out_specs=(rows, rows, rows),
        check_vma=False,
    )
```
